32 devices in a mesh: group: 2 (over x), expert: 8 (over z, y), dp: 2 (over core).
Axes of the slice: x: 2, y: 2, z: 4, core: 2. Of those that a mesh axis runs over, the one named last changes fastest.
Arguments:
- tokens: bfloat16 [4096, 3584], P(('group', 'expert', 'dp')), parts along dimension 0, may hold values from -6 to 6
- expert_ids: int32 [4096, 4], P(('group', 'expert', 'dp')), parts along dimension 0, may hold values from 0 to 7, as said below
- combine: float32 [4096, 4], P(('group', 'expert', 'dp')), parts along dimension 0, may hold values from 0.1 to 1
- hot_list: int32 [2], P('group'), parts along dimension 0, may hold values from 0 to 7, as said below
- in_weight: bfloat16 [8, 2, 3584, 1024], P('expert', None, None, 'dp'), may hold values from -0.09375 to 0.09375
- in_scale: float32 [8, 2, 28, 8], P('expert', None, None, 'dp'), may hold values from 0.5 to 2
- out_weight: bfloat16 [8, 1024, 3584], P('expert', 'dp'), may hold values from -0.1875 to 0.1875
- out_scale: float32 [8, 8, 28], P('expert', 'dp'), may hold values from 0.5 to 2
Outputs:
- mixed: bfloat16 [4096, 3584], P(('group', 'expert', 'dp')), parts along dimension 0
The draws below stay inside these ranges and needn't reach their ends.
There are 2 independent parts, one for each index of `group`. The reference program is written for one: setup_inputs(seed, part) draws one part's arguments, and reference() takes and returns one part's arrays. A program takes and returns all parts, laid end to end along the dimension named above; an argument that names none is the same for every part. Nothing has to cross between parts.
Inputs may be any that keep to these rules, and one draw needn't show every extreme that they name: `expert_ids`: each row names 4 different experts. `hot_list`: one expert per group, a valid expert id.
All inputs are finite; a program needn't handle non-finite values.
Results may differ from the reference program's by a relative error of at most 0.008.
Values may be sent and summed in bfloat16 or wider, within the bound.
No kernel may reach another device: no remote copies, remote signals or barrier semaphores. Data moves between devices by JAX's collectives and lax.ppermute only.
A program may use at most 192 MiB of HBM per device.

```python
import math
import jax
import jax.numpy as jnp
from jax import lax

D = 3584
F = 1024
QB = 128
TOP = 4
HOT = 1
TOK_DEV = 128
EXPERTS = 8
TOKENS = 2048
CAP = 48
N_EXPERT = 8
N_DP = 2


def routing_table(key):
    ordering = jax.random.permutation(jax.random.fold_in(key, 11), EXPERTS)
    hot_ids = ordering[:HOT].astype(jnp.int32)
    noise_ranks = jax.random.randint(jax.random.fold_in(key, 12), (TOKENS, EXPERTS), 0, 65536)
    favour = jax.random.randint(jax.random.fold_in(key, 13), (EXPERTS,), 0, 32768)
    lucky_rows = jax.random.randint(jax.random.fold_in(key, 14), (TOKENS, 1), 0, 4) < 3
    labels = jnp.arange(EXPERTS, dtype=jnp.int32)
    is_hot = jnp.any(labels[:, None] == hot_ids[None, :], axis=1)
    boosted = jnp.where(lucky_rows & is_hot[None, :], 131072, 0)
    scores = (noise_ranks + favour[None, :] + boosted) * EXPERTS + labels[None, :]
    chosen = lax.top_k(scores, TOP)[1].astype(jnp.int32)
    return (chosen, hot_ids)


def draw_expert_ids(key, part):
    shared = routing_table(key)
    return shared[0]


def draw_hot_list(key, part):
    shared = routing_table(key)
    return shared[1]


def shard_levels(key, shape, split, smallest, largest):
    factor_of = 1.0
    for dim, parts in split:
        heights = jax.random.uniform(jax.random.fold_in(jax.random.fold_in(key, 6), dim), (parts,), jnp.float32, smallest / len(split), largest / len(split))
        factor_of = factor_of * jnp.repeat(jnp.exp(heights), shape[dim] // parts).reshape((-1,) + (1,) * (len(shape) - 1 - dim))
    return factor_of


def normal_values(own_key, dims, scale, reach, pieces=(), held_as=jnp.bfloat16):
    loudness = shard_levels(own_key, dims, pieces, -0.22, 0.18) if pieces else 1.0
    result = jax.random.normal(own_key, dims, jnp.float32) * scale * loudness
    return jnp.minimum(jnp.maximum(result, -reach), reach).astype(held_as)


def setup_inputs(seed: int = 0, part: int = 0) -> dict:
    seeds = jax.random.split(jax.random.key(seed), 9)
    own_keys = jax.random.split(jax.random.fold_in(seeds[8], part), 9)
    return {
        "tokens": normal_values(own_keys[0], (TOKENS, D), 1.0, 6.0, ((0, 16),)),
        "expert_ids": draw_expert_ids(jax.random.fold_in(jax.random.fold_in(seeds[8], part), 71), part),
        "combine": jnp.clip(jnp.exp(math.log(1.0) - 2.3025851 * jax.random.uniform(own_keys[2], (TOKENS, TOP), jnp.float32) ** shard_levels(own_keys[2], (TOKENS, TOP), ((0, 16),), -0.2, 0.2)), 0.1, 1.0),
        "hot_list": draw_hot_list(jax.random.fold_in(jax.random.fold_in(seeds[8], part), 71), part),
        "in_weight": normal_values(seeds[4], (EXPERTS, 2, D, F), D ** -0.5, 0.09375, ((0, 8), (3, 2))),
        "in_scale": jnp.clip(jnp.exp(math.log(2.0) - 1.3862944 * jax.random.uniform(seeds[5], (EXPERTS, 2, D // QB, F // QB), jnp.float32) ** shard_levels(seeds[5], (EXPERTS, 2, D // QB, F // QB), ((0, 8), (3, 2)), -0.2, 0.2)), 0.5, 2.0),
        "out_weight": normal_values(seeds[6], (EXPERTS, F, D), F ** -0.5, 0.1875, ((0, 8), (1, 2))),
        "out_scale": jnp.clip(jnp.exp(math.log(2.0) - 1.3862944 * jax.random.uniform(seeds[7], (EXPERTS, F // QB, D // QB), jnp.float32) ** shard_levels(seeds[7], (EXPERTS, F // QB, D // QB), ((0, 8), (1, 2)), -0.2, 0.2)), 0.5, 2.0),
    }


def dequantize(raw_weight, raw_scale):
    array_shape = raw_weight.shape
    tiled = raw_weight.astype(jnp.float32).reshape(array_shape[:-2] + (array_shape[-2] // QB, QB, array_shape[-1] // QB, QB))
    return (tiled * raw_scale[..., :, None, :, None]).reshape(array_shape).astype(jnp.bfloat16)


def expert_part(source_rows, deq_in, deq_out):
    gate_value = jnp.dot(source_rows, deq_in[0], preferred_element_type=jnp.float32)
    up_value = jnp.dot(source_rows, deq_in[1], preferred_element_type=jnp.float32)
    hidden = (jax.nn.silu(gate_value) * up_value).astype(jnp.bfloat16)
    return jnp.dot(hidden, deq_out, preferred_element_type=jnp.float32).astype(jnp.bfloat16)


def reference(tokens, expert_ids, combine, hot_list, in_weight, in_scale, out_weight, out_scale):
    sources = N_EXPERT * N_DP
    hot_expert = hot_list[0]
    pair_ids = expert_ids.reshape(sources, TOK_DEV * TOP)
    labels = jnp.arange(EXPERTS, dtype=jnp.int32)
    one_hot = (pair_ids[:, :, None] == labels[None, None, :]).astype(jnp.int32)
    slot_rank = jnp.sum(jnp.cumsum(one_hot, axis=1) * one_hot, axis=2) - 1
    routed = (pair_ids != hot_expert) & (slot_rank < CAP)
    slot_index = jnp.where(routed, pair_ids * CAP + slot_rank, EXPERTS * CAP).astype(jnp.int32)
    picked = jnp.repeat(tokens.reshape(sources, TOK_DEV, D), TOP, axis=1)

    def fill_rows(slots_one, rows_one):
        return jnp.zeros((EXPERTS * CAP, D), tokens.dtype).at[slots_one].set(rows_one, mode="drop")

    buffers = jax.vmap(fill_rows)(slot_index, picked).reshape(sources, EXPERTS, CAP, D)

    def run_expert(expert_index):
        deq_in = dequantize(in_weight[expert_index], in_scale[expert_index])
        deq_out = dequantize(out_weight[expert_index], out_scale[expert_index])
        block_rows = buffers[:, expert_index].reshape(sources * CAP, D)
        return expert_part(block_rows, deq_in, deq_out)

    results = lax.map(run_expert, labels).reshape(EXPERTS, sources, CAP, D)
    shadow = expert_part(tokens, dequantize(in_weight[hot_expert], in_scale[hot_expert]), dequantize(out_weight[hot_expert], out_scale[hot_expert]))
    ids_grid = expert_ids.reshape(sources, TOK_DEV, TOP)
    rank_grid = jnp.clip(slot_rank, 0, CAP - 1).reshape(sources, TOK_DEV, TOP)
    routed_grid = routed.reshape(sources, TOK_DEV, TOP)
    weight_grid = combine.reshape(sources, TOK_DEV, TOP)
    source_index = jnp.broadcast_to(jnp.arange(sources, dtype=jnp.int32)[:, None], (sources, TOK_DEV))
    summed = jnp.zeros((sources, TOK_DEV, D), jnp.float32)
    shadow_weight = jnp.zeros((sources, TOK_DEV), jnp.float32)
    for column in range(TOP):
        chosen = ids_grid[:, :, column]
        pair_weight = jnp.where(routed_grid[:, :, column], weight_grid[:, :, column], jnp.zeros_like(weight_grid[:, :, column]))
        part_rows = results[chosen, source_index, rank_grid[:, :, column]]
        summed = summed + pair_weight[:, :, None] * part_rows.astype(jnp.float32)
        shadow_weight = shadow_weight + jnp.where(chosen == hot_expert, weight_grid[:, :, column], jnp.zeros_like(weight_grid[:, :, column]))
    summed = summed + shadow_weight[:, :, None] * shadow.astype(jnp.float32).reshape(sources, TOK_DEV, D)
    return summed.reshape(TOKENS, D).astype(jnp.bfloat16)
```

```python
import functools

import jax
import jax.numpy as jnp
from jax import lax
from jax.experimental import pallas as pl
from jax.experimental.pallas import tpu as pltpu
from jax.sharding import PartitionSpec as P

QB = 128
TILE_F = 256
VMEM_LIMIT = 56 * 1024 * 1024


def ring_order(mesh):
    count = mesh.shape["expert"]
    rows = 2 if count == 8 else 1
    first = [i * rows for i in range(count // rows)]
    second = [i * rows + 1 for i in reversed(range(count // rows))] if rows == 2 else []
    return first + second


def dequantize(raw_weight, raw_scale):
    shape = raw_weight.shape
    tiled = raw_weight.astype(jnp.float32).reshape(
        shape[:-2] + (shape[-2] // QB, QB, shape[-1] // QB, QB)
    )
    return (tiled * raw_scale[..., :, None, :, None]).reshape(shape).astype(jnp.bfloat16)


def route_kernel(capacity, hot_ref, ids_ref, combine_ref, out_ref):
    rows, owners = out_ref.shape
    ids = ids_ref[...]
    combine = combine_ref[...]
    lane = lax.broadcasted_iota(jnp.int32, (rows, owners), 1)
    named = jnp.zeros((rows, owners), jnp.float32)
    weight = jnp.zeros((rows, owners), jnp.float32)
    for k in range(ids.shape[1]):
        here = ids[:, k : k + 1] == lane
        named = named + jnp.where(here, 1.0, 0.0)
        weight = weight + jnp.where(here, combine[:, k : k + 1], 0.0)
    later = lax.broadcasted_iota(jnp.int32, (rows, rows), 0)
    earlier = lax.broadcasted_iota(jnp.int32, (rows, rows), 1)
    before = jnp.where(earlier < later, 1.0, 0.0).astype(jnp.bfloat16)
    rank = jnp.dot(before, named.astype(jnp.bfloat16), preferred_element_type=jnp.float32)
    keep = (lane == hot_ref[0]) | (rank < capacity)
    out_ref[...] = jnp.where(keep, weight, 0.0)


def route(hot_list, expert_ids, combine, owners, capacity):
    rows = expert_ids.shape[0]
    return pl.pallas_call(
        functools.partial(route_kernel, capacity),
        out_shape=jax.ShapeDtypeStruct((rows, owners), jnp.float32),
        in_specs=[
            pl.BlockSpec(memory_space=pltpu.SMEM),
            pl.BlockSpec(memory_space=pltpu.VMEM),
            pl.BlockSpec(memory_space=pltpu.VMEM),
        ],
        out_specs=pl.BlockSpec(memory_space=pltpu.VMEM),
        name="route",
    )(hot_list, expert_ids, combine)


def expert_kernel(sizes, half_steps, where_ref, weight_ref, in_own, out_own, in_sib, out_sib, *refs):
    blocks = len(sizes)
    x_refs, o_refs = refs[:blocks], refs[blocks : 2 * blocks]
    rows, total = refs[2 * blocks :]
    step = pl.program_id(0)
    starts = [sum(sizes[:i]) for i in range(blocks)]

    @pl.when(step == 0)
    def _():
        for start, size, x_ref in zip(starts, sizes, x_refs):
            rows[start : start + size, :] = x_ref[...]

    def add(in_ref, out_ref, first):
        x = rows[...]
        gate = jnp.dot(x, in_ref[0], preferred_element_type=jnp.float32)
        up = jnp.dot(x, in_ref[1], preferred_element_type=jnp.float32)
        hidden = (gate / (1.0 + jnp.exp(-gate)) * up).astype(jnp.bfloat16)
        term = jnp.dot(hidden, out_ref[...], preferred_element_type=jnp.float32)

        @pl.when(step == 0)
        def _():
            total[...] = term

        @pl.when(step != 0)
        def _():
            total[...] += term

    @pl.when(step < half_steps)
    def _():
        add(in_own, out_own, True)

    @pl.when(step >= half_steps)
    def _():
        add(in_sib, out_sib, False)

    @pl.when(step == 2 * half_steps - 1)
    def _():
        lane = lax.broadcasted_iota(jnp.int32, (8, weight_ref.shape[1]), 1)[0:1]
        for i, (start, size, o_ref) in enumerate(zip(starts, sizes, o_refs)):
            at = pl.multiple_of(where_ref[1 + i], 8)
            table = weight_ref[pl.ds(at, size), :]
            weight = jnp.sum(jnp.where(lane == where_ref[0], table, 0.0), axis=1, keepdims=True)
            o_ref[...] = (total[start : start + size, :] * weight).astype(jnp.bfloat16)


def run_expert(blocks, where, weights, own, sib):
    in_own, out_own = own
    in_sib, out_sib = sib
    width, half = in_own.shape[1], in_own.shape[2]
    half_steps = half // TILE_F
    sizes = tuple(b.shape[0] for b in blocks)
    m = sum(sizes)
    last = half_steps - 1
    whole = pl.BlockSpec(memory_space=pltpu.VMEM)
    return pl.pallas_call(
        functools.partial(expert_kernel, sizes, half_steps),
        grid=(2 * half_steps,),
        out_shape=[jax.ShapeDtypeStruct(b.shape, jnp.bfloat16) for b in blocks],
        in_specs=[
            pl.BlockSpec(memory_space=pltpu.SMEM),
            whole,
            pl.BlockSpec((2, width, TILE_F), lambda j: (0, 0, jnp.minimum(j, last))),
            pl.BlockSpec((TILE_F, width), lambda j: (jnp.minimum(j, last), 0)),
            pl.BlockSpec((2, width, TILE_F), lambda j: (0, 0, jnp.maximum(j - half_steps, 0))),
            pl.BlockSpec((TILE_F, width), lambda j: (jnp.maximum(j - half_steps, 0), 0)),
        ]
        + [whole] * len(blocks),
        out_specs=[whole] * len(blocks),
        scratch_shapes=[
            pltpu.VMEM((m, width), jnp.bfloat16),
            pltpu.VMEM((m, width), jnp.float32),
        ],
        compiler_params=pltpu.CompilerParams(vmem_limit_bytes=VMEM_LIMIT),
        cost_estimate=pl.CostEstimate(
            flops=2 * m * width * half * 6, bytes_accessed=6 * width * half * 2, transcendentals=0
        ),
        name="expert",
    )(where, weights, in_own, out_own, in_sib, out_sib, *blocks)


def shards(order, tokens, expert_ids, combine, hot_list, in_weight, in_scale, out_weight, out_scale):
    owners = lax.axis_size("expert")
    halves = lax.axis_size("dp")
    tok_rows, width = tokens.shape
    capacity = tok_rows * expert_ids.shape[1] * 3 // (4 * owners)
    mine = lax.axis_index("expert")
    far = owners // 2
    mid = tok_rows // 2

    def shift(x, by):
        return lax.ppermute(
            x, "expert", [(order[i], order[(i + by) % owners]) for i in range(owners)]
        )

    def add(a, b):
        return (a.astype(jnp.float32) + b.astype(jnp.float32)).astype(jnp.bfloat16)

    place = [order.index(i) for i in range(owners)]
    at = jnp.array(place, jnp.int32)[mine]
    around = jnp.array(order, jnp.int32)

    def source(by):
        return around[(at + by) % owners] * tok_rows

    own = (dequantize(in_weight[0], in_scale[0]), dequantize(out_weight[0], out_scale[0]))
    swap = [(i, (i + 1) % halves) for i in range(halves)]
    sib = tuple(lax.ppermute(w, "dp", swap) for w in own)

    weights = lax.all_gather(
        route(hot_list, expert_ids, combine, owners, capacity), "expert", axis=0, tiled=True
    )

    done = {}

    def expert(keys, blocks, offsets):
        where = jnp.stack([mine.astype(jnp.int32)] + [o.astype(jnp.int32) for o in offsets])
        for key, out in zip(keys, run_expert(blocks, where, weights, own, sib)):
            done[key] = out

    ahead = behind = tokens
    waiting = [("0", tokens, source(0))]
    for s in range(1, far):
        behind = shift(behind, 1)
        ahead = shift(ahead, -1)
        waiting += [(-s, behind, source(-s)), (s, ahead, source(s))]
        expert(*zip(*waiting))
        waiting = []
    top = shift(behind[:mid], 1)
    bottom = shift(ahead[mid:], -1)
    expert(("top", "bottom"), (top, bottom), (source(far), source(far) + mid))

    to_right = shift(done["top"], 1)
    to_left = shift(done["bottom"], -1)
    empty = jnp.zeros((mid, width), jnp.bfloat16)
    to_right = jnp.concatenate([to_right, empty], axis=0)
    to_left = jnp.concatenate([empty, to_left], axis=0)
    for s in range(far - 1, 0, -1):
        to_right = shift(add(done[s], to_right), 1)
        to_left = shift(add(done[-s], to_left), -1)
    own_rows = done["0"].astype(jnp.float32)
    return (own_rows + to_right.astype(jnp.float32) + to_left.astype(jnp.float32)).astype(
        jnp.bfloat16
    )


def solution(mesh):
    placed = (
        P(("group", "expert", "dp"), None),
        P(("group", "expert", "dp"), None),
        P(("group", "expert", "dp"), None),
        P("group"),
        P("expert", None, None, "dp"),
        P("expert", None, None, "dp"),
        P("expert", "dp", None),
        P("expert", "dp", None),
    )
    return jax.shard_map(
        functools.partial(shards, ring_order(mesh)),
        mesh=mesh,
        in_specs=placed,
        out_specs=P(("group", "expert", "dp"), None),
        check_vma=False,
    )
```

```python
import functools

import jax
import jax.numpy as jnp
from jax import lax
from jax.experimental import pallas as pl
from jax.experimental.pallas import tpu as pltpu
from jax.sharding import PartitionSpec as P

QB = 128
TILE_F = 256
LANES = 128
VMEM_LIMIT = 56 * 1024 * 1024
CHUNKS = 1
SCALE = 1.0


def cost(flops, bytes_accessed):
    return pl.CostEstimate(
        flops=int(flops * SCALE), bytes_accessed=int(bytes_accessed * SCALE), transcendentals=0
    )


def ring_order(mesh):
    count = mesh.shape["expert"]
    rows = 2 if count == 8 else 1
    first = [i * rows for i in range(count // rows)]
    second = [i * rows + 1 for i in reversed(range(count // rows))] if rows == 2 else []
    return first + second


def dequantize_kernel(in_scale, out_scale, in_raw, out_raw, out_ref):
    f, part = pl.program_id(0), pl.program_id(1)
    chunk = in_raw.shape[1]

    def scaled(block, scale):
        return (block.astype(jnp.float32) * scale).astype(jnp.bfloat16)

    @pl.when(part < 2)
    def _():
        for side in range(2):
            for i in range(chunk // QB):
                for j in range(TILE_F // QB):
                    scale = in_scale[side, part * (chunk // QB) + i, f * (TILE_F // QB) + j]
                    at = side * TILE_F + j * QB
                    out_ref[0, i * QB : (i + 1) * QB, at : at + QB] = scaled(
                        in_raw[side, i * QB : (i + 1) * QB, j * QB : (j + 1) * QB], scale
                    )

    @pl.when(part == 2)
    def _():
        per = 2 * TILE_F // QB
        for i in range(TILE_F // QB):
            for j in range(out_raw.shape[1] // QB):
                scale = out_scale[f * (TILE_F // QB) + i, j]
                row, at = (j // per) * TILE_F + i * QB, (j % per) * QB
                out_ref[0, row : row + QB, at : at + QB] = scaled(
                    out_raw[i * QB : (i + 1) * QB, j * QB : (j + 1) * QB], scale
                )


def dequantize(in_raw, in_scale, out_raw, out_scale):
    width, half = in_raw.shape[1], in_raw.shape[2]
    tiles = half // TILE_F
    chunk = width // 2
    return pl.pallas_call(
        dequantize_kernel,
        grid=(tiles, 3),
        out_shape=jax.ShapeDtypeStruct((tiles, 3 * chunk, 2 * TILE_F), jnp.bfloat16),
        in_specs=[
            pl.BlockSpec(memory_space=pltpu.SMEM),
            pl.BlockSpec(memory_space=pltpu.SMEM),
            pl.BlockSpec((2, chunk, TILE_F), lambda f, p: (0, jnp.minimum(p, 1), f)),
            pl.BlockSpec((TILE_F, width), lambda f, p: (f, 0)),
        ],
        out_specs=pl.BlockSpec((1, chunk, 2 * TILE_F), lambda f, p: (f, p, 0)),
        compiler_params=pltpu.CompilerParams(vmem_limit_bytes=VMEM_LIMIT),
        cost_estimate=cost(6 * width * half, 12 * width * half),
        name="dequantize",
    )(in_scale, out_scale, in_raw, out_raw)


def route_kernel(capacity, owners, hot_ref, ids_ref, combine_ref, tokens_ref, *out_refs):
    picks, rows = ids_ref.shape
    expert = lax.broadcasted_iota(jnp.int32, (owners, rows), 0)
    named = jnp.zeros((owners, rows), jnp.float32)
    weight = jnp.zeros((owners, rows), jnp.float32)
    for k in range(picks):
        here = ids_ref[k : k + 1, :] == expert
        named = named + jnp.where(here, 1.0, 0.0)
        weight = weight + jnp.where(here, combine_ref[k : k + 1, :], 0.0)
    earlier = lax.broadcasted_iota(jnp.int32, (rows, rows), 0)
    later = lax.broadcasted_iota(jnp.int32, (rows, rows), 1)
    before = jnp.where(earlier < later, 1.0, 0.0).astype(jnp.bfloat16)
    rank = jnp.dot(named.astype(jnp.bfloat16), before, preferred_element_type=jnp.float32)
    weight = jnp.where((expert == hot_ref[0]) | (rank < capacity), weight, 0.0)
    pieces = []
    for _ in range(3):
        piece = weight.astype(jnp.bfloat16).astype(jnp.float32)
        weight = weight - piece
        pieces.append(piece)
    pieces.append(jnp.zeros((LANES - 3 * owners, rows), jnp.float32))
    extra = jnp.concatenate(pieces, axis=0).T.astype(jnp.bfloat16)
    width = tokens_ref.shape[1]
    size = rows // len(out_refs)
    for c, out_ref in enumerate(out_refs):
        out_ref[:, :width] = tokens_ref[c * size : (c + 1) * size, :]
        out_ref[:, width:] = extra[c * size : (c + 1) * size, :]


def route(hot_list, expert_ids, combine, tokens, owners, capacity):
    rows, width = tokens.shape
    vmem = pl.BlockSpec(memory_space=pltpu.VMEM)
    return pl.pallas_call(
        functools.partial(route_kernel, capacity, owners),
        out_shape=[jax.ShapeDtypeStruct((rows // CHUNKS, width + LANES), jnp.bfloat16)] * CHUNKS,
        in_specs=[pl.BlockSpec(memory_space=pltpu.SMEM), vmem, vmem, vmem],
        out_specs=[vmem] * CHUNKS,
        name="route",
    )(hot_list, expert_ids.T, combine.T, tokens)


def expert_kernel(sizes, owners, who_ref, own, sib, *refs):
    blocks = len(sizes)
    x_refs, o_refs = refs[:blocks], refs[blocks : 2 * blocks]
    rows, total, held, arrived = refs[2 * blocks :]
    starts = [sum(sizes[:i]) for i in range(blocks)]
    half_tiles, width = own.shape[0], rows.shape[1]
    tiles = 2 * half_tiles
    cut = width // 2

    def copies(ref, at, tile):
        return [
            pltpu.make_async_copy(
                ref.at[at, pl.ds(part * cut, cut)],
                held.at[tile, pl.ds(part * cut, cut)],
                arrived.at[tile, part],
            )
            for part in range(3)
        ]

    landed = []
    for tile in range(tiles):
        half = own if tile < half_tiles else sib
        landed.append(copies(half, tile % half_tiles, tile))
        for copy in landed[-1]:
            copy.start()
    for start, size, x_ref in zip(starts, sizes, x_refs):
        rows[start : start + size, :] = x_ref[:, :width]

    for tile in range(tiles):
        landed[tile][0].wait()
        both = jnp.dot(rows[:, :cut], held[tile, :cut], preferred_element_type=jnp.float32)
        landed[tile][1].wait()
        both += jnp.dot(
            rows[:, cut:], held[tile, cut : 2 * cut], preferred_element_type=jnp.float32
        )
        gate, up = both[:, :TILE_F], both[:, TILE_F:]
        hidden = (gate / (1.0 + jnp.exp(-gate)) * up).astype(jnp.bfloat16)
        landed[tile][2].wait()
        for i in range(width // (2 * TILE_F)):
            at = slice(i * 2 * TILE_F, (i + 1) * 2 * TILE_F)
            term = jnp.dot(
                hidden,
                held[tile, width + i * TILE_F : width + (i + 1) * TILE_F],
                preferred_element_type=jnp.float32,
            )
            total[:, at] = term if tile == 0 else total[:, at] + term
    for start, size, x_ref, o_ref in zip(starts, sizes, x_refs, o_refs):
        lane = lax.broadcasted_iota(jnp.int32, (size, LANES), 1)
        picked = (lax.rem(lane, owners) == who_ref[0]) & (lane < 3 * owners)
        weight = jnp.where(picked, x_ref[:, width:].astype(jnp.float32), 0.0)
        weight = jnp.sum(weight, axis=1, keepdims=True)
        o_ref[...] = (total[start : start + size, :] * weight).astype(jnp.bfloat16)


def run_expert(blocks, owners, who, own, sib):
    tiles, width = own.shape[0], blocks[0].shape[1] - LANES
    sizes = tuple(x.shape[0] for x in blocks)
    m = sum(sizes)
    whole = pl.BlockSpec(memory_space=pltpu.VMEM)
    return pl.pallas_call(
        functools.partial(expert_kernel, sizes, owners),
        out_shape=[jax.ShapeDtypeStruct((size, width), jnp.bfloat16) for size in sizes],
        in_specs=[pl.BlockSpec(memory_space=pltpu.SMEM)]
        + [pl.BlockSpec(memory_space=pl.ANY)] * 2
        + [whole] * len(blocks),
        out_specs=[whole] * len(blocks),
        scratch_shapes=[
            pltpu.VMEM((m, width), jnp.bfloat16),
            pltpu.VMEM((m, width), jnp.float32),
            pltpu.VMEM((2 * tiles,) + own.shape[1:], jnp.bfloat16),
            pltpu.SemaphoreType.DMA((2 * tiles, 3)),
        ],
        compiler_params=pltpu.CompilerParams(vmem_limit_bytes=VMEM_LIMIT),
        cost_estimate=cost(12 * m * width * tiles * TILE_F, 12 * width * tiles * TILE_F),
        name="expert",
    )(who, own, sib, *blocks)


def after(value, *others):
    return lax.optimization_barrier((value, others))[0]


def shards(order, tokens, expert_ids, combine, hot_list, in_weight, in_scale, out_weight, out_scale):
    owners = lax.axis_size("expert")
    halves = lax.axis_size("dp")
    tok_rows, width = tokens.shape
    capacity = tok_rows * expert_ids.shape[1] * 3 // (4 * owners)
    who = lax.axis_index("expert").astype(jnp.int32).reshape(1)
    far = owners // 2
    size = tok_rows // CHUNKS
    mid = size // 2
    chunks = range(CHUNKS)

    def shift(x, by):
        return lax.ppermute(
            x, "expert", [(order[i], order[(i + by) % owners]) for i in range(owners)]
        )

    def add(a, b):
        return (a.astype(jnp.float32) + b.astype(jnp.float32)).astype(jnp.bfloat16)

    have = [{0: x} for x in route(hot_list, expert_ids, combine, tokens, owners, capacity)]
    done = [{} for _ in chunks]

    def gather(c, s):
        if s < far:
            have[c][-s] = shift(have[c][1 - s], 1)
            have[c][s] = shift(have[c][s - 1], -1)
        else:
            have[c]["top"] = shift(have[c][1 - s][:mid], 1)
            have[c]["bottom"] = shift(have[c][s - 1][mid:], -1)

    def expert(*keys):
        blocks = [have[c][key] for c, key in keys]
        for (c, key), out in zip(keys, run_expert(blocks, owners, who, own, sib)):
            done[c][key] = out

    def hold(keys, *others):
        for c, key in keys:
            have[c][key] = after(have[c][key], *others)

    def every(*steps):
        return [(c, key) for s in steps for c in chunks for key in ((s, -s) if s else (0,))]

    for c in chunks:
        gather(c, 1)
    own = dequantize(
        *after((in_weight[0], in_scale[0], out_weight[0], out_scale[0]), have[0][0])
    )
    halved = after(own, [have[c][key] for c, key in every(1)])
    sib = lax.ppermute(halved, "dp", [(i, (i + 1) % halves) for i in range(halves)])
    for c in chunks:
        gather(c, 2)
    for s in range(2, far):
        for c in chunks:
            gather(c, s + 1)
        expert(*every(s))
        if s + 1 < far:
            hold(every(s + 1), done[0][s])
        else:
            hold([(c, key) for c in chunks for key in ("top", "bottom")], done[0][s])
    for c in chunks:
        expert((c, "top"), (c, "bottom"))

    right, left = [None] * CHUNKS, [None] * CHUNKS
    empty = jnp.zeros((mid, width), jnp.bfloat16)
    for c in chunks:
        right[c] = shift(done[c]["top"], 1)
        left[c] = shift(done[c]["bottom"], -1)
    hold(every(0), [done[c]["top"] for c in chunks])
    expert(*every(0))
    hold(every(1), right, left, done[0][0])
    for c in chunks:
        right[c] = jnp.concatenate([right[c], empty], axis=0)
        left[c] = jnp.concatenate([empty, left[c]], axis=0)
    for s in range(far - 1, 0, -1):
        for c in chunks:
            right[c] = shift(add(done[c][s], right[c]), 1)
            left[c] = shift(add(done[c][-s], left[c]), -1)
        if s == far - 1:
            expert(*every(1))
    mixed = [
        (
            done[c][0].astype(jnp.float32)
            + right[c].astype(jnp.float32)
            + left[c].astype(jnp.float32)
        ).astype(jnp.bfloat16)
        for c in chunks
    ]
    return jnp.concatenate(mixed, axis=0) if CHUNKS > 1 else mixed[0]


def solution(mesh):
    placed = (
        P(("group", "expert", "dp"), None),
        P(("group", "expert", "dp"), None),
        P(("group", "expert", "dp"), None),
        P("group"),
        P("expert", None, None, "dp"),
        P("expert", None, None, "dp"),
        P("expert", "dp", None),
        P("expert", "dp", None),
    )
    return jax.shard_map(
        functools.partial(shards, ring_order(mesh)),
        mesh=mesh,
        in_specs=placed,
        out_specs=P(("group", "expert", "dp"), None),
        check_vma=False,
    )
```

```python
import functools

import jax
import jax.numpy as jnp
from jax import lax
from jax.experimental import pallas as pl
from jax.experimental.pallas import tpu as pltpu
from jax.sharding import PartitionSpec as P

QB = 128
TILE_F = 256
LANES = 128
VMEM_LIMIT = 56 * 1024 * 1024
CHUNKS = 1
SCALE = 1.0


def cost(flops, bytes_accessed):
    return pl.CostEstimate(
        flops=int(flops * SCALE), bytes_accessed=int(bytes_accessed * SCALE), transcendentals=0
    )


def ring_order(mesh):
    count = mesh.shape["expert"]
    rows = 2 if count == 8 else 1
    first = [i * rows for i in range(count // rows)]
    second = [i * rows + 1 for i in reversed(range(count // rows))] if rows == 2 else []
    return first + second


def dequantize_kernel(in_scale, out_scale, in_raw, out_raw, out_ref):
    f, part = pl.program_id(0), pl.program_id(1)
    chunk = in_raw.shape[1]

    def scaled(block, scale):
        return (block.astype(jnp.float32) * scale).astype(jnp.bfloat16)

    @pl.when(part < 2)
    def _():
        for side in range(2):
            for i in range(chunk // QB):
                for j in range(TILE_F // QB):
                    scale = in_scale[side, part * (chunk // QB) + i, f * (TILE_F // QB) + j]
                    at = side * TILE_F + j * QB
                    out_ref[0, i * QB : (i + 1) * QB, at : at + QB] = scaled(
                        in_raw[side, i * QB : (i + 1) * QB, j * QB : (j + 1) * QB], scale
                    )

    @pl.when(part == 2)
    def _():
        per = 2 * TILE_F // QB
        for i in range(TILE_F // QB):
            for j in range(out_raw.shape[1] // QB):
                scale = out_scale[f * (TILE_F // QB) + i, j]
                row, at = (j // per) * TILE_F + i * QB, (j % per) * QB
                out_ref[0, row : row + QB, at : at + QB] = scaled(
                    out_raw[i * QB : (i + 1) * QB, j * QB : (j + 1) * QB], scale
                )


def dequantize(in_raw, in_scale, out_raw, out_scale):
    width, half = in_raw.shape[1], in_raw.shape[2]
    tiles = half // TILE_F
    chunk = width // 2
    return pl.pallas_call(
        dequantize_kernel,
        grid=(tiles, 3),
        out_shape=jax.ShapeDtypeStruct((tiles, 3 * chunk, 2 * TILE_F), jnp.bfloat16),
        in_specs=[
            pl.BlockSpec(memory_space=pltpu.SMEM),
            pl.BlockSpec(memory_space=pltpu.SMEM),
            pl.BlockSpec((2, chunk, TILE_F), lambda f, p: (0, jnp.minimum(p, 1), f)),
            pl.BlockSpec((TILE_F, width), lambda f, p: (f, 0)),
        ],
        out_specs=pl.BlockSpec((1, chunk, 2 * TILE_F), lambda f, p: (f, p, 0)),
        compiler_params=pltpu.CompilerParams(vmem_limit_bytes=24 * 1024 * 1024),
        cost_estimate=cost(6 * width * half, 12 * width * half),
        name="dequantize",
    )(in_scale, out_scale, in_raw, out_raw)


def route_kernel(capacity, owners, hot_ref, ids_ref, combine_ref, tokens_ref, *out_refs):
    picks, rows = ids_ref.shape
    expert = lax.broadcasted_iota(jnp.int32, (owners, rows), 0)
    named = jnp.zeros((owners, rows), jnp.float32)
    weight = jnp.zeros((owners, rows), jnp.float32)
    for k in range(picks):
        here = ids_ref[k : k + 1, :] == expert
        named = named + jnp.where(here, 1.0, 0.0)
        weight = weight + jnp.where(here, combine_ref[k : k + 1, :], 0.0)
    earlier = lax.broadcasted_iota(jnp.int32, (rows, rows), 0)
    later = lax.broadcasted_iota(jnp.int32, (rows, rows), 1)
    before = jnp.where(earlier < later, 1.0, 0.0).astype(jnp.bfloat16)
    rank = jnp.dot(named.astype(jnp.bfloat16), before, preferred_element_type=jnp.float32)
    weight = jnp.where((expert == hot_ref[0]) | (rank < capacity), weight, 0.0)
    pieces = []
    for _ in range(3):
        piece = weight.astype(jnp.bfloat16).astype(jnp.float32)
        weight = weight - piece
        pieces.append(piece)
    pieces.append(jnp.zeros((LANES - 3 * owners, rows), jnp.float32))
    extra = jnp.concatenate(pieces, axis=0).T.astype(jnp.bfloat16)
    width = tokens_ref.shape[1]
    size = rows // len(out_refs)
    for c, out_ref in enumerate(out_refs):
        out_ref[:, :width] = tokens_ref[c * size : (c + 1) * size, :]
        out_ref[:, width:] = extra[c * size : (c + 1) * size, :]


def route(hot_list, expert_ids, combine, tokens, owners, capacity):
    rows, width = tokens.shape
    vmem = pl.BlockSpec(memory_space=pltpu.VMEM)
    return pl.pallas_call(
        functools.partial(route_kernel, capacity, owners),
        out_shape=[jax.ShapeDtypeStruct((rows // CHUNKS, width + LANES), jnp.bfloat16)] * CHUNKS,
        in_specs=[pl.BlockSpec(memory_space=pltpu.SMEM), vmem, vmem, vmem],
        out_specs=[vmem] * CHUNKS,
        name="route",
    )(hot_list, expert_ids.T, combine.T, tokens)


def expert_kernel(sizes, owners, who_ref, own, sib, *refs):
    blocks = len(sizes)
    x_refs, o_refs = refs[:blocks], refs[blocks : 2 * blocks]
    rows, total = refs[2 * blocks :]
    starts = [sum(sizes[:i]) for i in range(blocks)]
    half_tiles, width = own.shape[0], rows.shape[1]
    tiles = 2 * half_tiles
    for start, size, x_ref in zip(starts, sizes, x_refs):
        rows[start : start + size, :] = x_ref[:, :width]

    for tile in range(tiles):
        held, at = (own, tile) if tile < half_tiles else (sib, tile - half_tiles)
        both = jnp.dot(rows[...], held[at, :width], preferred_element_type=jnp.float32)
        gate, up = both[:, :TILE_F], both[:, TILE_F:]
        hidden = (gate / (1.0 + jnp.exp(-gate)) * up).astype(jnp.bfloat16)
        for i in range(width // (2 * TILE_F)):
            to = slice(i * 2 * TILE_F, (i + 1) * 2 * TILE_F)
            term = jnp.dot(
                hidden,
                held[at, width + i * TILE_F : width + (i + 1) * TILE_F],
                preferred_element_type=jnp.float32,
            )
            total[:, to] = term if tile == 0 else total[:, to] + term
    for start, size, x_ref, o_ref in zip(starts, sizes, x_refs, o_refs):
        lane = lax.broadcasted_iota(jnp.int32, (size, LANES), 1)
        picked = (lax.rem(lane, owners) == who_ref[0]) & (lane < 3 * owners)
        weight = jnp.where(picked, x_ref[:, width:].astype(jnp.float32), 0.0)
        weight = jnp.sum(weight, axis=1, keepdims=True)
        o_ref[...] = (total[start : start + size, :] * weight).astype(jnp.bfloat16)


def keep_kernel(own_from, sib_from, own_to, sib_to, arrived):
    copies = []
    for side, (from_ref, to_ref) in enumerate(((own_from, own_to), (sib_from, sib_to))):
        for tile in range(from_ref.shape[0]):
            copies.append(
                pltpu.make_async_copy(
                    from_ref.at[tile], to_ref.at[tile], arrived.at[side, tile]
                )
            )
    for copy in copies:
        copy.start()
    for copy in copies:
        copy.wait()


def keep(own, sib):
    held = pl.pallas_call(
        keep_kernel,
        out_shape=[pltpu.VMEM(own.shape, own.dtype)] * 2,
        in_specs=[pl.BlockSpec(memory_space=pl.ANY)] * 2,
        out_specs=[pl.BlockSpec(memory_space=pltpu.VMEM)] * 2,
        scratch_shapes=[pltpu.SemaphoreType.DMA((2, own.shape[0]))],
        compiler_params=pltpu.CompilerParams(vmem_limit_bytes=2 * 1024 * 1024),
        name="keep",
    )(own, sib)
    return [pltpu.with_memory_space_constraint(h, pltpu.VMEM) for h in held]


def run_expert(blocks, owners, who, own, sib):
    tiles, width = own.shape[0], blocks[0].shape[1] - LANES
    sizes = tuple(x.shape[0] for x in blocks)
    m = sum(sizes)
    whole = pl.BlockSpec(memory_space=pltpu.VMEM)
    return pl.pallas_call(
        functools.partial(expert_kernel, sizes, owners),
        out_shape=[jax.ShapeDtypeStruct((size, width), jnp.bfloat16) for size in sizes],
        in_specs=[pl.BlockSpec(memory_space=pltpu.SMEM)]
        + [whole] * (2 + len(blocks)),
        out_specs=[whole] * len(blocks),
        scratch_shapes=[
            pltpu.VMEM((m, width), jnp.bfloat16),
            pltpu.VMEM((m, width), jnp.float32),
        ],
        compiler_params=pltpu.CompilerParams(vmem_limit_bytes=24 * 1024 * 1024),
        cost_estimate=cost(12 * m * width * tiles * TILE_F, 12 * width * tiles * TILE_F),
        name="expert",
    )(who, own, sib, *blocks)


def after(value, *others):
    return lax.optimization_barrier((value, others))[0]


def shards(order, tokens, expert_ids, combine, hot_list, in_weight, in_scale, out_weight, out_scale):
    owners = lax.axis_size("expert")
    halves = lax.axis_size("dp")
    tok_rows, width = tokens.shape
    capacity = tok_rows * expert_ids.shape[1] * 3 // (4 * owners)
    who = lax.axis_index("expert").astype(jnp.int32).reshape(1)
    far = owners // 2
    size = tok_rows // CHUNKS
    mid = size // 2
    chunks = range(CHUNKS)

    def shift(x, by):
        return lax.ppermute(
            x, "expert", [(order[i], order[(i + by) % owners]) for i in range(owners)]
        )

    def add(a, b):
        return (a.astype(jnp.float32) + b.astype(jnp.float32)).astype(jnp.bfloat16)

    have = [{0: x} for x in route(hot_list, expert_ids, combine, tokens, owners, capacity)]
    done = [{} for _ in chunks]

    def gather(c, s):
        if s < far:
            have[c][-s] = shift(have[c][1 - s], 1)
            have[c][s] = shift(have[c][s - 1], -1)
        else:
            have[c]["top"] = shift(have[c][1 - s][:mid], 1)
            have[c]["bottom"] = shift(have[c][s - 1][mid:], -1)

    def expert(*keys):
        blocks = [have[c][key] for c, key in keys]
        for (c, key), out in zip(keys, run_expert(blocks, owners, who, own, sib)):
            done[c][key] = out

    def hold(keys, *others):
        for c, key in keys:
            have[c][key] = after(have[c][key], *others)

    def every(*steps):
        return [(c, key) for s in steps for c in chunks for key in ((s, -s) if s else (0,))]

    for c in chunks:
        gather(c, 1)
    own = dequantize(
        *after((in_weight[0], in_scale[0], out_weight[0], out_scale[0]), have[0][0])
    )
    halved = after(own, [have[c][key] for c, key in every(1)])
    sib = lax.ppermute(halved, "dp", [(i, (i + 1) % halves) for i in range(halves)])
    for c in chunks:
        gather(c, 2)
    own, sib = keep(own, sib)
    for s in range(2, far):
        for c in chunks:
            gather(c, s + 1)
        expert(*every(s))
        if s + 1 < far:
            hold(every(s + 1), done[0][s])
        else:
            hold([(c, key) for c in chunks for key in ("top", "bottom")], done[0][s])
    for c in chunks:
        expert((c, "top"), (c, "bottom"))

    right, left = [None] * CHUNKS, [None] * CHUNKS
    empty = jnp.zeros((mid, width), jnp.bfloat16)
    for c in chunks:
        right[c] = shift(done[c]["top"], 1)
        left[c] = shift(done[c]["bottom"], -1)
    hold(every(0), [done[c]["top"] for c in chunks])
    expert(*every(0))
    hold(every(1), right, left, done[0][0])
    for c in chunks:
        right[c] = jnp.concatenate([right[c], empty], axis=0)
        left[c] = jnp.concatenate([empty, left[c]], axis=0)
    for s in range(far - 1, 0, -1):
        for c in chunks:
            right[c] = shift(add(done[c][s], right[c]), 1)
            left[c] = shift(add(done[c][-s], left[c]), -1)
        if s == far - 1:
            expert(*every(1))
    mixed = [
        (
            done[c][0].astype(jnp.float32)
            + right[c].astype(jnp.float32)
            + left[c].astype(jnp.float32)
        ).astype(jnp.bfloat16)
        for c in chunks
    ]
    return jnp.concatenate(mixed, axis=0) if CHUNKS > 1 else mixed[0]


def solution(mesh):
    placed = (
        P(("group", "expert", "dp"), None),
        P(("group", "expert", "dp"), None),
        P(("group", "expert", "dp"), None),
        P("group"),
        P("expert", None, None, "dp"),
        P("expert", None, None, "dp"),
        P("expert", "dp", None),
        P("expert", "dp", None),
    )
    return jax.shard_map(
        functools.partial(shards, ring_order(mesh)),
        mesh=mesh,
        in_specs=placed,
        out_specs=P(("group", "expert", "dp"), None),
        check_vma=False,
    )
```

```python
import functools

import jax
import jax.numpy as jnp
from jax import lax
from jax.experimental import pallas as pl
from jax.experimental.pallas import tpu as pltpu
from jax.sharding import PartitionSpec as P

QB = 128
TILE_F = 256
LANES = 128
VMEM_LIMIT = 56 * 1024 * 1024
CHUNKS = 1
SCALE = 1.0


def cost(flops, bytes_accessed):
    return pl.CostEstimate(
        flops=int(flops * SCALE), bytes_accessed=int(bytes_accessed * SCALE), transcendentals=0
    )


def ring_order(mesh):
    count = mesh.shape["expert"]
    rows = 2 if count == 8 else 1
    first = [i * rows for i in range(count // rows)]
    second = [i * rows + 1 for i in reversed(range(count // rows))] if rows == 2 else []
    return first + second


def dequantize_kernel(in_scale, out_scale, in_raw, out_raw, out_ref):
    f, part = pl.program_id(0), pl.program_id(1)
    chunk = in_raw.shape[1]

    def scaled(block, scale):
        return (block.astype(jnp.float32) * scale).astype(jnp.bfloat16)

    @pl.when(part < 2)
    def _():
        for side in range(2):
            for i in range(chunk // QB):
                for j in range(TILE_F // QB):
                    scale = in_scale[side, part * (chunk // QB) + i, f * (TILE_F // QB) + j]
                    at = side * TILE_F + j * QB
                    out_ref[0, i * QB : (i + 1) * QB, at : at + QB] = scaled(
                        in_raw[side, i * QB : (i + 1) * QB, j * QB : (j + 1) * QB], scale
                    )

    @pl.when(part == 2)
    def _():
        per = 2 * TILE_F // QB
        for i in range(TILE_F // QB):
            for j in range(out_raw.shape[1] // QB):
                scale = out_scale[f * (TILE_F // QB) + i, j]
                row, at = (j // per) * TILE_F + i * QB, (j % per) * QB
                out_ref[0, row : row + QB, at : at + QB] = scaled(
                    out_raw[i * QB : (i + 1) * QB, j * QB : (j + 1) * QB], scale
                )


def dequantize(in_raw, in_scale, out_raw, out_scale):
    width, half = in_raw.shape[1], in_raw.shape[2]
    tiles = half // TILE_F
    chunk = width // 2
    return pl.pallas_call(
        dequantize_kernel,
        grid=(tiles, 3),
        out_shape=jax.ShapeDtypeStruct((tiles, 3 * chunk, 2 * TILE_F), jnp.bfloat16),
        in_specs=[
            pl.BlockSpec(memory_space=pltpu.SMEM),
            pl.BlockSpec(memory_space=pltpu.SMEM),
            pl.BlockSpec((2, chunk, TILE_F), lambda f, p: (0, jnp.minimum(p, 1), f)),
            pl.BlockSpec((TILE_F, width), lambda f, p: (f, 0)),
        ],
        out_specs=pl.BlockSpec((1, chunk, 2 * TILE_F), lambda f, p: (f, p, 0)),
        compiler_params=pltpu.CompilerParams(vmem_limit_bytes=24 * 1024 * 1024),
        cost_estimate=cost(6 * width * half, 12 * width * half),
        name="dequantize",
    )(in_scale, out_scale, in_raw, out_raw)


def route_kernel(capacity, owners, hot_ref, ids_ref, combine_ref, tokens_ref, *out_refs):
    picks, rows = ids_ref.shape
    expert = lax.broadcasted_iota(jnp.int32, (owners, rows), 0)
    named = jnp.zeros((owners, rows), jnp.float32)
    weight = jnp.zeros((owners, rows), jnp.float32)
    for k in range(picks):
        here = ids_ref[k : k + 1, :] == expert
        named = named + jnp.where(here, 1.0, 0.0)
        weight = weight + jnp.where(here, combine_ref[k : k + 1, :], 0.0)
    earlier = lax.broadcasted_iota(jnp.int32, (rows, rows), 0)
    later = lax.broadcasted_iota(jnp.int32, (rows, rows), 1)
    before = jnp.where(earlier < later, 1.0, 0.0).astype(jnp.bfloat16)
    rank = jnp.dot(named.astype(jnp.bfloat16), before, preferred_element_type=jnp.float32)
    weight = jnp.where((expert == hot_ref[0]) | (rank < capacity), weight, 0.0)
    pieces = []
    for _ in range(3):
        piece = weight.astype(jnp.bfloat16).astype(jnp.float32)
        weight = weight - piece
        pieces.append(piece)
    pieces.append(jnp.zeros((LANES - 3 * owners, rows), jnp.float32))
    extra = jnp.concatenate(pieces, axis=0).T.astype(jnp.bfloat16)
    width = tokens_ref.shape[1]
    size = rows // len(out_refs)
    for c, out_ref in enumerate(out_refs):
        out_ref[:, :width] = tokens_ref[c * size : (c + 1) * size, :]
        out_ref[:, width:] = extra[c * size : (c + 1) * size, :]


def route(hot_list, expert_ids, combine, tokens, owners, capacity):
    rows, width = tokens.shape
    vmem = pl.BlockSpec(memory_space=pltpu.VMEM)
    return pl.pallas_call(
        functools.partial(route_kernel, capacity, owners),
        out_shape=[jax.ShapeDtypeStruct((rows // CHUNKS, width + LANES), jnp.bfloat16)] * CHUNKS,
        in_specs=[pl.BlockSpec(memory_space=pltpu.SMEM), vmem, vmem, vmem],
        out_specs=[vmem] * CHUNKS,
        name="route",
    )(hot_list, expert_ids.T, combine.T, tokens)


def expert_kernel(sizes, owners, who_ref, own, sib, *refs):
    blocks = len(sizes)
    x_refs, o_refs = refs[:blocks], refs[blocks : 2 * blocks]
    rows, total = refs[2 * blocks :]
    starts = [sum(sizes[:i]) for i in range(blocks)]
    half_tiles, width = own.shape[0], rows.shape[1]
    tiles = 2 * half_tiles
    for start, size, x_ref in zip(starts, sizes, x_refs):
        rows[start : start + size, :] = x_ref[:, :width]

    for tile in range(tiles):
        held, at = (own, tile) if tile < half_tiles else (sib, tile - half_tiles)
        both = jnp.dot(rows[...], held[at, :width], preferred_element_type=jnp.float32)
        gate, up = both[:, :TILE_F], both[:, TILE_F:]
        hidden = (gate / (1.0 + jnp.exp(-gate)) * up).astype(jnp.bfloat16)
        for i in range(width // (2 * TILE_F)):
            to = slice(i * 2 * TILE_F, (i + 1) * 2 * TILE_F)
            term = jnp.dot(
                hidden,
                held[at, width + i * TILE_F : width + (i + 1) * TILE_F],
                preferred_element_type=jnp.float32,
            )
            total[:, to] = term if tile == 0 else total[:, to] + term
    for start, size, x_ref, o_ref in zip(starts, sizes, x_refs, o_refs):
        lane = lax.broadcasted_iota(jnp.int32, (size, LANES), 1)
        picked = (lax.rem(lane, owners) == who_ref[0]) & (lane < 3 * owners)
        weight = jnp.where(picked, x_ref[:, width:].astype(jnp.float32), 0.0)
        weight = jnp.sum(weight, axis=1, keepdims=True)
        o_ref[...] = (total[start : start + size, :] * weight).astype(jnp.bfloat16)


def keep_kernel(
    in_scale, out_scale, own_from, in_raw, out_raw, own_to, sib_to, in_here, out_here, own_sem, in_sem, out_sem
):
    tiles, width = own_from.shape[0], in_raw.shape[1]
    parts = 4
    chunk = width // parts

    def in_copy(part):
        rows = pl.ds(pl.multiple_of(part * chunk, QB), chunk)
        return pltpu.make_async_copy(in_raw.at[:, rows], in_here.at[:, rows], in_sem.at[part])

    out_copy = pltpu.make_async_copy(out_raw, out_here, out_sem)
    own_copies = [
        pltpu.make_async_copy(own_from.at[tile], own_to.at[tile], own_sem.at[tile])
        for tile in range(tiles)
    ]
    for part in range(parts):
        in_copy(part).start()
    out_copy.start()
    for copy in own_copies:
        copy.start()

    def scaled(block, scale):
        return (block.astype(jnp.float32) * scale).astype(jnp.bfloat16)

    def gate_up(part, carry):
        in_copy(part).wait()
        for i in range(chunk // QB):
            row = part * (chunk // QB) + i
            rows = pl.ds(pl.multiple_of(row * QB, QB), QB)
            for side in range(2):
                for j in range(tiles * TILE_F // QB):
                    tile, at = (j * QB) // TILE_F, side * TILE_F + (j * QB) % TILE_F
                    sib_to[tile, rows, at : at + QB] = scaled(
                        in_here[side, rows, j * QB : (j + 1) * QB], in_scale[side, row, j]
                    )
        return carry

    lax.fori_loop(0, parts, gate_up, 0)
    out_copy.wait()
    per = 2 * TILE_F // QB
    below = TILE_F // QB

    def down(i, carry):
        rows = pl.ds(pl.multiple_of(i * QB, QB), QB)
        for j in range(width // QB):
            to = width + (j // per) * TILE_F + lax.rem(i, below) * QB
            at = (j % per) * QB
            sib_to[lax.div(i, below), pl.ds(pl.multiple_of(to, QB), QB), at : at + QB] = scaled(
                out_here[rows, j * QB : (j + 1) * QB], out_scale[i, j]
            )
        return carry

    lax.fori_loop(0, tiles * below, down, 0)
    for copy in own_copies:
        copy.wait()


def keep(own, in_raw, in_scale, out_raw, out_scale):
    smem = pl.BlockSpec(memory_space=pltpu.SMEM)
    held = pl.pallas_call(
        keep_kernel,
        out_shape=[pltpu.VMEM(own.shape, own.dtype)] * 2,
        in_specs=[smem, smem] + [pl.BlockSpec(memory_space=pl.ANY)] * 3,
        out_specs=[pl.BlockSpec(memory_space=pltpu.VMEM)] * 2,
        scratch_shapes=[
            pltpu.VMEM(in_raw.shape, in_raw.dtype),
            pltpu.VMEM(out_raw.shape, out_raw.dtype),
            pltpu.SemaphoreType.DMA((own.shape[0],)),
            pltpu.SemaphoreType.DMA((4,)),
            pltpu.SemaphoreType.DMA(()),
        ],
        compiler_params=pltpu.CompilerParams(vmem_limit_bytes=14 * 1024 * 1024),
        name="keep",
    )(in_scale, out_scale, own, in_raw, out_raw)
    return [pltpu.with_memory_space_constraint(h, pltpu.VMEM) for h in held]


def run_expert(blocks, owners, who, own, sib):
    tiles, width = own.shape[0], blocks[0].shape[1] - LANES
    sizes = tuple(x.shape[0] for x in blocks)
    m = sum(sizes)
    whole = pl.BlockSpec(memory_space=pltpu.VMEM)
    return pl.pallas_call(
        functools.partial(expert_kernel, sizes, owners),
        out_shape=[jax.ShapeDtypeStruct((size, width), jnp.bfloat16) for size in sizes],
        in_specs=[pl.BlockSpec(memory_space=pltpu.SMEM)]
        + [whole] * (2 + len(blocks)),
        out_specs=[whole] * len(blocks),
        scratch_shapes=[
            pltpu.VMEM((m, width), jnp.bfloat16),
            pltpu.VMEM((m, width), jnp.float32),
        ],
        compiler_params=pltpu.CompilerParams(vmem_limit_bytes=24 * 1024 * 1024),
        cost_estimate=cost(12 * m * width * tiles * TILE_F, 12 * width * tiles * TILE_F),
        name="expert",
    )(who, own, sib, *blocks)


def after(value, *others):
    return lax.optimization_barrier((value, others))[0]


def shards(order, tokens, expert_ids, combine, hot_list, in_weight, in_scale, out_weight, out_scale):
    owners = lax.axis_size("expert")
    halves = lax.axis_size("dp")
    tok_rows, width = tokens.shape
    capacity = tok_rows * expert_ids.shape[1] * 3 // (4 * owners)
    who = lax.axis_index("expert").astype(jnp.int32).reshape(1)
    far = owners // 2
    size = tok_rows // CHUNKS
    mid = size // 2
    chunks = range(CHUNKS)

    def shift(x, by, name):
        with jax.named_scope(name + ("_right" if by > 0 else "_left")):
            return lax.ppermute(
                x, "expert", [(order[i], order[(i + by) % owners]) for i in range(owners)]
            )

    def add(a, b):
        return (a.astype(jnp.float32) + b.astype(jnp.float32)).astype(jnp.bfloat16)

    have = [{0: x} for x in route(hot_list, expert_ids, combine, tokens, owners, capacity)]
    done = [{} for _ in chunks]

    def gather(c, s):
        if s < far:
            have[c][-s] = shift(have[c][1 - s], 1, f"tokens_{c}_{s}")
            have[c][s] = shift(have[c][s - 1], -1, f"tokens_{c}_{s}")
        else:
            have[c]["top"] = shift(have[c][1 - s][:mid], 1, f"tokens_{c}_{s}")
            have[c]["bottom"] = shift(have[c][s - 1][mid:], -1, f"tokens_{c}_{s}")

    def expert(*keys):
        blocks = [have[c][key] for c, key in keys]
        for (c, key), out in zip(keys, run_expert(blocks, owners, who, own, sib)):
            done[c][key] = out

    def hold(keys, *others):
        for c, key in keys:
            have[c][key] = after(have[c][key], *others)

    def every(*steps):
        return [(c, key) for s in steps for c in chunks for key in ((s, -s) if s else (0,))]

    for c in chunks:
        gather(c, 1)
    raw = (in_weight[0], in_scale[0], out_weight[0], out_scale[0])
    sizes = jnp.concatenate([raw[1].reshape(-1), raw[3].reshape(-1)])
    in_sib, out_sib, sizes = [
        lax.ppermute(w, "dp", [(i, (i + 1) % halves) for i in range(halves)])
        for w in (raw[0], raw[2], sizes)
    ]
    own = dequantize(*after(raw, have[0][0]))
    for s in range(2, far):
        for c in chunks:
            if s == 2:
                hold([(c, 1), (c, -1)], own)
            gather(c, s)
    cut = raw[1].size
    own, sib = keep(
        own, in_sib, sizes[:cut].reshape(raw[1].shape), out_sib, sizes[cut:].reshape(raw[3].shape)
    )
    hold(every(far - 1), own)
    for c in chunks:
        gather(c, far)
        expert((c, far - 1), (c, 1 - far))
        hold([(c, "top"), (c, "bottom")], done[c][far - 1])

    right, left = [None] * CHUNKS, [None] * CHUNKS
    empty = jnp.zeros((mid, width), jnp.bfloat16)
    for c in chunks:
        expert((c, "top"), (c, "bottom"))
        right[c] = shift(done[c]["top"], 1, f"sums_{c}_{far}")
        left[c] = shift(done[c]["bottom"], -1, f"sums_{c}_{far}")
    for c in chunks:
        right[c] = jnp.concatenate([right[c], empty], axis=0)
        left[c] = jnp.concatenate([empty, left[c]], axis=0)
    for s in range(far - 1, 0, -1):
        for c in chunks:
            keys = [(c, s - 1), (c, 1 - s)] if s > 1 else []
            if s == 2:
                keys.append((c, 0))
            if keys:
                hold(keys, right[c], left[c])
            right[c] = shift(add(done[c][s], right[c]), 1, f"sums_{c}_{s}")
            left[c] = shift(add(done[c][-s], left[c]), -1, f"sums_{c}_{s}")
            if keys:
                expert(*keys)
    mixed = [
        (
            done[c][0].astype(jnp.float32)
            + right[c].astype(jnp.float32)
            + left[c].astype(jnp.float32)
        ).astype(jnp.bfloat16)
        for c in chunks
    ]
    return jnp.concatenate(mixed, axis=0) if CHUNKS > 1 else mixed[0]


def solution(mesh):
    placed = (
        P(("group", "expert", "dp"), None),
        P(("group", "expert", "dp"), None),
        P(("group", "expert", "dp"), None),
        P("group"),
        P("expert", None, None, "dp"),
        P("expert", None, None, "dp"),
        P("expert", "dp", None),
        P("expert", "dp", None),
    )
    return jax.shard_map(
        functools.partial(shards, ring_order(mesh)),
        mesh=mesh,
        in_specs=placed,
        out_specs=P(("group", "expert", "dp"), None),
        check_vma=False,
    )
```

```python
import functools

import jax
import jax.numpy as jnp
from jax import lax
from jax.experimental import pallas as pl
from jax.experimental.pallas import tpu as pltpu
from jax.sharding import PartitionSpec as P

QB = 128
TILE_F = 256
LANES = 128
VMEM_LIMIT = 56 * 1024 * 1024
CHUNKS = 1
SCALE = 1.0


def cost(flops, bytes_accessed):
    return pl.CostEstimate(
        flops=int(flops * SCALE), bytes_accessed=int(bytes_accessed * SCALE), transcendentals=0
    )


def ring_order(mesh):
    count = mesh.shape["expert"]
    rows = 2 if count == 8 else 1
    first = [i * rows for i in range(count // rows)]
    second = [i * rows + 1 for i in reversed(range(count // rows))] if rows == 2 else []
    return first + second


def dequantize_kernel(in_scale, out_scale, in_raw, out_raw, out_ref):
    f, part = pl.program_id(0), pl.program_id(1)
    chunk = in_raw.shape[1]

    def scaled(block, scale):
        return (block.astype(jnp.float32) * scale).astype(jnp.bfloat16)

    @pl.when(part < 2)
    def _():
        for side in range(2):
            for i in range(chunk // QB):
                for j in range(TILE_F // QB):
                    scale = in_scale[side, part * (chunk // QB) + i, f * (TILE_F // QB) + j]
                    at = side * TILE_F + j * QB
                    out_ref[0, i * QB : (i + 1) * QB, at : at + QB] = scaled(
                        in_raw[side, i * QB : (i + 1) * QB, j * QB : (j + 1) * QB], scale
                    )

    @pl.when(part == 2)
    def _():
        per = 2 * TILE_F // QB
        for i in range(TILE_F // QB):
            for j in range(out_raw.shape[1] // QB):
                scale = out_scale[f * (TILE_F // QB) + i, j]
                row, at = (j // per) * TILE_F + i * QB, (j % per) * QB
                out_ref[0, row : row + QB, at : at + QB] = scaled(
                    out_raw[i * QB : (i + 1) * QB, j * QB : (j + 1) * QB], scale
                )


def dequantize(in_raw, in_scale, out_raw, out_scale):
    width, half = in_raw.shape[1], in_raw.shape[2]
    tiles = half // TILE_F
    chunk = width // 2
    return pl.pallas_call(
        dequantize_kernel,
        grid=(tiles, 3),
        out_shape=jax.ShapeDtypeStruct((tiles, 3 * chunk, 2 * TILE_F), jnp.bfloat16),
        in_specs=[
            pl.BlockSpec(memory_space=pltpu.SMEM),
            pl.BlockSpec(memory_space=pltpu.SMEM),
            pl.BlockSpec((2, chunk, TILE_F), lambda f, p: (0, jnp.minimum(p, 1), f)),
            pl.BlockSpec((TILE_F, width), lambda f, p: (f, 0)),
        ],
        out_specs=pl.BlockSpec((1, chunk, 2 * TILE_F), lambda f, p: (f, p, 0)),
        compiler_params=pltpu.CompilerParams(vmem_limit_bytes=24 * 1024 * 1024),
        cost_estimate=cost(6 * width * half, 12 * width * half),
        name="dequantize",
    )(in_scale, out_scale, in_raw, out_raw)


def route_kernel(capacity, owners, hot_ref, ids_ref, combine_ref, tokens_ref, *out_refs):
    picks, rows = ids_ref.shape
    expert = lax.broadcasted_iota(jnp.int32, (owners, rows), 0)
    named = jnp.zeros((owners, rows), jnp.float32)
    weight = jnp.zeros((owners, rows), jnp.float32)
    for k in range(picks):
        here = ids_ref[k : k + 1, :] == expert
        named = named + jnp.where(here, 1.0, 0.0)
        weight = weight + jnp.where(here, combine_ref[k : k + 1, :], 0.0)
    earlier = lax.broadcasted_iota(jnp.int32, (rows, rows), 0)
    later = lax.broadcasted_iota(jnp.int32, (rows, rows), 1)
    before = jnp.where(earlier < later, 1.0, 0.0).astype(jnp.bfloat16)
    rank = jnp.dot(named.astype(jnp.bfloat16), before, preferred_element_type=jnp.float32)
    weight = jnp.where((expert == hot_ref[0]) | (rank < capacity), weight, 0.0)
    pieces = []
    for _ in range(3):
        piece = weight.astype(jnp.bfloat16).astype(jnp.float32)
        weight = weight - piece
        pieces.append(piece)
    pieces.append(jnp.zeros((LANES - 3 * owners, rows), jnp.float32))
    extra = jnp.concatenate(pieces, axis=0).T.astype(jnp.bfloat16)
    width = tokens_ref.shape[1]
    size = rows // len(out_refs)
    for c, out_ref in enumerate(out_refs):
        out_ref[:, :width] = tokens_ref[c * size : (c + 1) * size, :]
        out_ref[:, width:] = extra[c * size : (c + 1) * size, :]


def route(hot_list, expert_ids, combine, tokens, owners, capacity):
    rows, width = tokens.shape
    vmem = pl.BlockSpec(memory_space=pltpu.VMEM)
    return pl.pallas_call(
        functools.partial(route_kernel, capacity, owners),
        out_shape=[jax.ShapeDtypeStruct((rows // CHUNKS, width + LANES), jnp.bfloat16)] * CHUNKS,
        in_specs=[pl.BlockSpec(memory_space=pltpu.SMEM), vmem, vmem, vmem],
        out_specs=[vmem] * CHUNKS,
        name="route",
    )(hot_list, expert_ids.T, combine.T, tokens)


def expert_kernel(sizes, owners, who_ref, own, sib, *refs):
    blocks = len(sizes)
    x_refs, o_refs = refs[:blocks], refs[blocks : 2 * blocks]
    rows, total = refs[2 * blocks :]
    starts = [sum(sizes[:i]) for i in range(blocks)]
    half_tiles, width = own.shape[0], rows.shape[1]
    tiles = 2 * half_tiles
    for start, size, x_ref in zip(starts, sizes, x_refs):
        rows[start : start + size, :] = x_ref[:, :width]

    for tile in range(tiles):
        held, at = (own, tile) if tile < half_tiles else (sib, tile - half_tiles)
        both = jnp.dot(rows[...], held[at, :width], preferred_element_type=jnp.float32)
        gate, up = both[:, :TILE_F], both[:, TILE_F:]
        hidden = (gate / (1.0 + jnp.exp(-gate)) * up).astype(jnp.bfloat16)
        for i in range(width // (2 * TILE_F)):
            to = slice(i * 2 * TILE_F, (i + 1) * 2 * TILE_F)
            term = jnp.dot(
                hidden,
                held[at, width + i * TILE_F : width + (i + 1) * TILE_F],
                preferred_element_type=jnp.float32,
            )
            total[:, to] = term if tile == 0 else total[:, to] + term
    for start, size, x_ref, o_ref in zip(starts, sizes, x_refs, o_refs):
        lane = lax.broadcasted_iota(jnp.int32, (size, LANES), 1)
        picked = (lax.rem(lane, owners) == who_ref[0]) & (lane < 3 * owners)
        weight = jnp.where(picked, x_ref[:, width:].astype(jnp.float32), 0.0)
        weight = jnp.sum(weight, axis=1, keepdims=True)
        o_ref[...] = (total[start : start + size, :] * weight).astype(jnp.bfloat16)


def keep_kernel(
    in_scale, out_scale, own_from, in_raw, out_raw, own_to, sib_to, in_here, out_here, own_sem, in_sem, out_sem
):
    tiles, width = own_from.shape[0], in_raw.shape[1]
    parts = 4
    chunk = width // parts

    def in_copy(part):
        rows = pl.ds(pl.multiple_of(part * chunk, QB), chunk)
        return pltpu.make_async_copy(in_raw.at[:, rows], in_here.at[:, rows], in_sem.at[part])

    out_copy = pltpu.make_async_copy(out_raw, out_here, out_sem)
    own_copies = [
        pltpu.make_async_copy(own_from.at[tile], own_to.at[tile], own_sem.at[tile])
        for tile in range(tiles)
    ]
    for part in range(parts):
        in_copy(part).start()
    out_copy.start()
    for copy in own_copies:
        copy.start()

    def scaled(block, scale):
        return (block.astype(jnp.float32) * scale).astype(jnp.bfloat16)

    def gate_up(part, carry):
        in_copy(part).wait()
        for i in range(chunk // QB):
            row = part * (chunk // QB) + i
            rows = pl.ds(pl.multiple_of(row * QB, QB), QB)
            for side in range(2):
                for j in range(tiles * TILE_F // QB):
                    tile, at = (j * QB) // TILE_F, side * TILE_F + (j * QB) % TILE_F
                    sib_to[tile, rows, at : at + QB] = scaled(
                        in_here[side, rows, j * QB : (j + 1) * QB], in_scale[side, row, j]
                    )
        return carry

    lax.fori_loop(0, parts, gate_up, 0)
    out_copy.wait()
    per = 2 * TILE_F // QB
    below = TILE_F // QB

    def down(i, carry):
        rows = pl.ds(pl.multiple_of(i * QB, QB), QB)
        for j in range(width // QB):
            to = width + (j // per) * TILE_F + lax.rem(i, below) * QB
            at = (j % per) * QB
            sib_to[lax.div(i, below), pl.ds(pl.multiple_of(to, QB), QB), at : at + QB] = scaled(
                out_here[rows, j * QB : (j + 1) * QB], out_scale[i, j]
            )
        return carry

    lax.fori_loop(0, tiles * below, down, 0)
    for copy in own_copies:
        copy.wait()


def keep(own, in_raw, in_scale, out_raw, out_scale):
    smem = pl.BlockSpec(memory_space=pltpu.SMEM)
    held = pl.pallas_call(
        keep_kernel,
        out_shape=[pltpu.VMEM(own.shape, own.dtype)] * 2,
        in_specs=[smem, smem] + [pl.BlockSpec(memory_space=pl.ANY)] * 3,
        out_specs=[pl.BlockSpec(memory_space=pltpu.VMEM)] * 2,
        scratch_shapes=[
            pltpu.VMEM(in_raw.shape, in_raw.dtype),
            pltpu.VMEM(out_raw.shape, out_raw.dtype),
            pltpu.SemaphoreType.DMA((own.shape[0],)),
            pltpu.SemaphoreType.DMA((4,)),
            pltpu.SemaphoreType.DMA(()),
        ],
        compiler_params=pltpu.CompilerParams(vmem_limit_bytes=14 * 1024 * 1024),
        name="keep",
    )(in_scale, out_scale, own, in_raw, out_raw)
    return [pltpu.with_memory_space_constraint(h, pltpu.VMEM) for h in held]


def run_expert(blocks, owners, who, own, sib):
    tiles, width = own.shape[0], blocks[0].shape[1] - LANES
    sizes = tuple(x.shape[0] for x in blocks)
    m = sum(sizes)
    whole = pl.BlockSpec(memory_space=pltpu.VMEM)
    return pl.pallas_call(
        functools.partial(expert_kernel, sizes, owners),
        out_shape=[jax.ShapeDtypeStruct((size, width), jnp.bfloat16) for size in sizes],
        in_specs=[pl.BlockSpec(memory_space=pltpu.SMEM)]
        + [whole] * (2 + len(blocks)),
        out_specs=[whole] * len(blocks),
        scratch_shapes=[
            pltpu.VMEM((m, width), jnp.bfloat16),
            pltpu.VMEM((m, width), jnp.float32),
        ],
        compiler_params=pltpu.CompilerParams(vmem_limit_bytes=24 * 1024 * 1024),
        cost_estimate=cost(12 * m * width * tiles * TILE_F, 12 * width * tiles * TILE_F),
        name="expert",
    )(who, own, sib, *blocks)


def after(value, *others):
    return lax.optimization_barrier((value, others))[0]


def shards(order, tokens, expert_ids, combine, hot_list, in_weight, in_scale, out_weight, out_scale):
    owners = lax.axis_size("expert")
    halves = lax.axis_size("dp")
    tok_rows, width = tokens.shape
    capacity = tok_rows * expert_ids.shape[1] * 3 // (4 * owners)
    who = lax.axis_index("expert").astype(jnp.int32).reshape(1)
    far = owners // 2
    size = tok_rows // CHUNKS
    mid = size // 2
    chunks = range(CHUNKS)

    def shift(x, by, name):
        with jax.named_scope(name + ("_right" if by > 0 else "_left")):
            return lax.ppermute(
                x, "expert", [(order[i], order[(i + by) % owners]) for i in range(owners)]
            )

    def add(a, b):
        return (a.astype(jnp.float32) + b.astype(jnp.float32)).astype(jnp.bfloat16)

    have = [{0: x} for x in route(hot_list, expert_ids, combine, tokens, owners, capacity)]
    done = [{} for _ in chunks]

    def gather(c, s):
        if s < far:
            have[c][-s] = shift(have[c][1 - s], 1, f"tokens_{c}_{s}")
            have[c][s] = shift(have[c][s - 1], -1, f"tokens_{c}_{s}")
        else:
            have[c]["top"] = shift(have[c][1 - s][:mid], 1, f"tokens_{c}_{s}")
            have[c]["bottom"] = shift(have[c][s - 1][mid:], -1, f"tokens_{c}_{s}")

    def expert(*keys):
        blocks = [have[c][key] for c, key in keys]
        for (c, key), out in zip(keys, run_expert(blocks, owners, who, own, sib)):
            done[c][key] = out

    def hold(keys, *others):
        for c, key in keys:
            have[c][key] = after(have[c][key], *others)

    def every(*steps):
        return [(c, key) for s in steps for c in chunks for key in ((s, -s) if s else (0,))]

    for c in chunks:
        gather(c, 1)
    raw = (in_weight[0], in_scale[0], out_weight[0], out_scale[0])
    sizes = jnp.concatenate([raw[1].reshape(-1), raw[3].reshape(-1)])
    in_sib, out_sib, sizes = [
        lax.ppermute(w, "dp", [(i, (i + 1) % halves) for i in range(halves)])
        for w in (raw[0], raw[2], sizes)
    ]
    own = dequantize(*after(raw, have[0][0]))
    for s in range(2, far):
        for c in chunks:
            if s == 2:
                hold([(c, 1), (c, -1)], own)
            gather(c, s)
    cut = raw[1].size
    own, sib = keep(
        own, in_sib, sizes[:cut].reshape(raw[1].shape), out_sib, sizes[cut:].reshape(raw[3].shape)
    )
    hold(every(far - 1), own)
    gather(0, far)
    expert((0, far - 1), (0, 1 - far))
    hold([(0, "top"), (0, "bottom")], done[0][far - 1])
    expert((0, "top"), (0, "bottom"))

    part = done[0]
    right_low = shift(part[far - 1][mid:], 1, f"sums_1_{far - 1}")
    left_top = shift(part[1 - far][:mid], -1, f"sums_1_{far - 1}")
    right_top = shift(part["top"], 1, f"sums_0_{far}")
    left_low = shift(part["bottom"], -1, f"sums_0_{far}")
    before = part["top"]
    for s in range(far - 1, 1, -1):
        keys = [(0, s - 1), (0, 1 - s)] + ([(0, 0)] if s == 2 else [])
        hold(keys, before)
        expert(*keys)
        before = right_top
        right = jnp.concatenate(
            [add(part[s][:mid], right_top), add(part[s - 1][mid:], right_low)], axis=0
        )
        left = jnp.concatenate(
            [add(part[1 - s][:mid], left_top), add(part[-s][mid:], left_low)], axis=0
        )
        right, left = shift(right, 1, f"sums_0_{s}"), shift(left, -1, f"sums_0_{s}")
        right_top, right_low = right[:mid], right[mid:]
        left_top, left_low = left[:mid], left[mid:]
    right_top = shift(add(part[1][:mid], right_top), 1, "sums_0_1")
    left_low = shift(add(part[-1][mid:], left_low), -1, "sums_0_1")

    def three(*terms):
        return sum(t.astype(jnp.float32) for t in terms).astype(jnp.bfloat16)

    return jnp.concatenate(
        [
            three(part[0][:mid], right_top, left_top),
            three(part[0][mid:], right_low, left_low),
        ],
        axis=0,
    )


def solution(mesh):
    placed = (
        P(("group", "expert", "dp"), None),
        P(("group", "expert", "dp"), None),
        P(("group", "expert", "dp"), None),
        P("group"),
        P("expert", None, None, "dp"),
        P("expert", None, None, "dp"),
        P("expert", "dp", None),
        P("expert", "dp", None),
    )
    return jax.shard_map(
        functools.partial(shards, ring_order(mesh)),
        mesh=mesh,
        in_specs=placed,
        out_specs=P(("group", "expert", "dp"), None),
        check_vma=False,
    )
```

```python
import functools

import jax
import jax.numpy as jnp
from jax import lax
from jax.experimental import pallas as pl
from jax.experimental.pallas import tpu as pltpu
from jax.sharding import PartitionSpec as P

QB = 128
TILE_F = 256
LANES = 128
VMEM_LIMIT = 56 * 1024 * 1024
CHUNKS = 1
SCALE = 1.0


def cost(flops, bytes_accessed):
    return pl.CostEstimate(
        flops=int(flops * SCALE), bytes_accessed=int(bytes_accessed * SCALE), transcendentals=0
    )


def ring_order(mesh):
    count = mesh.shape["expert"]
    rows = 2 if count == 8 else 1
    first = [i * rows for i in range(count // rows)]
    second = [i * rows + 1 for i in reversed(range(count // rows))] if rows == 2 else []
    return first + second


def dequantize_kernel(in_scale, out_scale, in_raw, out_raw, out_ref):
    f, part = pl.program_id(0), pl.program_id(1)
    chunk = in_raw.shape[1]

    def scaled(block, scale):
        return (block.astype(jnp.float32) * scale).astype(jnp.bfloat16)

    @pl.when(part < 2)
    def _():
        for side in range(2):
            for i in range(chunk // QB):
                for j in range(TILE_F // QB):
                    scale = in_scale[side, part * (chunk // QB) + i, f * (TILE_F // QB) + j]
                    at = side * TILE_F + j * QB
                    out_ref[0, i * QB : (i + 1) * QB, at : at + QB] = scaled(
                        in_raw[side, i * QB : (i + 1) * QB, j * QB : (j + 1) * QB], scale
                    )

    @pl.when(part == 2)
    def _():
        per = 2 * TILE_F // QB
        for i in range(TILE_F // QB):
            for j in range(out_raw.shape[1] // QB):
                scale = out_scale[f * (TILE_F // QB) + i, j]
                row, at = (j // per) * TILE_F + i * QB, (j % per) * QB
                out_ref[0, row : row + QB, at : at + QB] = scaled(
                    out_raw[i * QB : (i + 1) * QB, j * QB : (j + 1) * QB], scale
                )


def dequantize(in_raw, in_scale, out_raw, out_scale):
    width, half = in_raw.shape[1], in_raw.shape[2]
    tiles = half // TILE_F
    chunk = width // 2
    return pl.pallas_call(
        dequantize_kernel,
        grid=(tiles, 3),
        out_shape=jax.ShapeDtypeStruct((tiles, 3 * chunk, 2 * TILE_F), jnp.bfloat16),
        in_specs=[
            pl.BlockSpec(memory_space=pltpu.SMEM),
            pl.BlockSpec(memory_space=pltpu.SMEM),
            pl.BlockSpec((2, chunk, TILE_F), lambda f, p: (0, jnp.minimum(p, 1), f)),
            pl.BlockSpec((TILE_F, width), lambda f, p: (f, 0)),
        ],
        out_specs=pl.BlockSpec((1, chunk, 2 * TILE_F), lambda f, p: (f, p, 0)),
        compiler_params=pltpu.CompilerParams(vmem_limit_bytes=24 * 1024 * 1024),
        cost_estimate=cost(6 * width * half, 12 * width * half),
        name="dequantize",
    )(in_scale, out_scale, in_raw, out_raw)


def route_kernel(capacity, owners, hot_ref, ids_ref, combine_ref, out_ref):
    picks, rows = ids_ref.shape
    expert = lax.broadcasted_iota(jnp.int32, (owners, rows), 0)
    named = jnp.zeros((owners, rows), jnp.float32)
    weight = jnp.zeros((owners, rows), jnp.float32)
    for k in range(picks):
        here = ids_ref[k : k + 1, :] == expert
        named = named + jnp.where(here, 1.0, 0.0)
        weight = weight + jnp.where(here, combine_ref[k : k + 1, :], 0.0)
    earlier = lax.broadcasted_iota(jnp.int32, (rows, rows), 0)
    later = lax.broadcasted_iota(jnp.int32, (rows, rows), 1)
    before = jnp.where(earlier < later, 1.0, 0.0).astype(jnp.bfloat16)
    rank = jnp.dot(named.astype(jnp.bfloat16), before, preferred_element_type=jnp.float32)
    weight = jnp.where((expert == hot_ref[0]) | (rank < capacity), weight, 0.0)
    pieces = []
    for _ in range(3):
        piece = weight.astype(jnp.bfloat16).astype(jnp.float32)
        weight = weight - piece
        pieces.append(piece)
    pieces.append(jnp.zeros((LANES - 3 * owners, rows), jnp.float32))
    extra = jnp.concatenate(pieces, axis=0).T.astype(jnp.bfloat16)
    out_ref[...] = extra


def route(hot_list, expert_ids, combine, owners, capacity):
    rows = expert_ids.shape[0]
    vmem = pl.BlockSpec(memory_space=pltpu.VMEM)
    return pl.pallas_call(
        functools.partial(route_kernel, capacity, owners),
        out_shape=jax.ShapeDtypeStruct((rows, LANES), jnp.bfloat16),
        in_specs=[pl.BlockSpec(memory_space=pltpu.SMEM), vmem, vmem],
        out_specs=vmem,
        name="route",
    )(hot_list, expert_ids.T, combine.T)


def expert_kernel(sizes, owners, who_ref, own, sib, *refs):
    blocks = len(sizes)
    x_refs, o_refs = refs[:blocks], refs[blocks : 2 * blocks]
    rows, total = refs[2 * blocks :]
    starts = [sum(sizes[:i]) for i in range(blocks)]
    half_tiles, width = own.shape[0], rows.shape[1]
    tiles = 2 * half_tiles
    for start, size, x_ref in zip(starts, sizes, x_refs):
        rows[start : start + size, :] = x_ref[:, :width]

    for tile in range(tiles):
        held, at = (own, tile) if tile < half_tiles else (sib, tile - half_tiles)
        both = jnp.dot(rows[...], held[at, :width], preferred_element_type=jnp.float32)
        gate, up = both[:, :TILE_F], both[:, TILE_F:]
        hidden = (gate / (1.0 + jnp.exp(-gate)) * up).astype(jnp.bfloat16)
        for i in range(width // (2 * TILE_F)):
            to = slice(i * 2 * TILE_F, (i + 1) * 2 * TILE_F)
            term = jnp.dot(
                hidden,
                held[at, width + i * TILE_F : width + (i + 1) * TILE_F],
                preferred_element_type=jnp.float32,
            )
            total[:, to] = term if tile == 0 else total[:, to] + term
    for start, size, x_ref, o_ref in zip(starts, sizes, x_refs, o_refs):
        lane = lax.broadcasted_iota(jnp.int32, (size, LANES), 1)
        picked = (lax.rem(lane, owners) == who_ref[0]) & (lane < 3 * owners)
        weight = jnp.where(picked, x_ref[:, width:].astype(jnp.float32), 0.0)
        weight = jnp.sum(weight, axis=1, keepdims=True)
        o_ref[...] = (total[start : start + size, :] * weight).astype(jnp.bfloat16)


def keep_kernel(
    in_scale, out_scale, own_from, in_raw, out_raw, own_to, sib_to, in_here, out_here, own_sem, in_sem, out_sem
):
    tiles, width = own_from.shape[0], in_raw.shape[1]
    parts = 4
    chunk = width // parts

    def in_copy(part):
        rows = pl.ds(pl.multiple_of(part * chunk, QB), chunk)
        return pltpu.make_async_copy(in_raw.at[:, rows], in_here.at[:, rows], in_sem.at[part])

    out_copy = pltpu.make_async_copy(out_raw, out_here, out_sem)
    own_copies = [
        pltpu.make_async_copy(own_from.at[tile], own_to.at[tile], own_sem.at[tile])
        for tile in range(tiles)
    ]
    for part in range(parts):
        in_copy(part).start()
    out_copy.start()
    for copy in own_copies:
        copy.start()

    def scaled(block, scale):
        return (block.astype(jnp.float32) * scale).astype(jnp.bfloat16)

    def gate_up(part, carry):
        in_copy(part).wait()
        for i in range(chunk // QB):
            row = part * (chunk // QB) + i
            rows = pl.ds(pl.multiple_of(row * QB, QB), QB)
            for side in range(2):
                for j in range(tiles * TILE_F // QB):
                    tile, at = (j * QB) // TILE_F, side * TILE_F + (j * QB) % TILE_F
                    sib_to[tile, rows, at : at + QB] = scaled(
                        in_here[side, rows, j * QB : (j + 1) * QB], in_scale[side, row, j]
                    )
        return carry

    lax.fori_loop(0, parts, gate_up, 0)
    out_copy.wait()
    per = 2 * TILE_F // QB
    below = TILE_F // QB

    def down(i, carry):
        rows = pl.ds(pl.multiple_of(i * QB, QB), QB)
        for j in range(width // QB):
            to = width + (j // per) * TILE_F + lax.rem(i, below) * QB
            at = (j % per) * QB
            sib_to[lax.div(i, below), pl.ds(pl.multiple_of(to, QB), QB), at : at + QB] = scaled(
                out_here[rows, j * QB : (j + 1) * QB], out_scale[i, j]
            )
        return carry

    lax.fori_loop(0, tiles * below, down, 0)
    for copy in own_copies:
        copy.wait()


def keep(own, in_raw, in_scale, out_raw, out_scale):
    smem = pl.BlockSpec(memory_space=pltpu.SMEM)
    held = pl.pallas_call(
        keep_kernel,
        out_shape=[pltpu.VMEM(own.shape, own.dtype)] * 2,
        in_specs=[smem, smem] + [pl.BlockSpec(memory_space=pl.ANY)] * 3,
        out_specs=[pl.BlockSpec(memory_space=pltpu.VMEM)] * 2,
        scratch_shapes=[
            pltpu.VMEM(in_raw.shape, in_raw.dtype),
            pltpu.VMEM(out_raw.shape, out_raw.dtype),
            pltpu.SemaphoreType.DMA((own.shape[0],)),
            pltpu.SemaphoreType.DMA((4,)),
            pltpu.SemaphoreType.DMA(()),
        ],
        compiler_params=pltpu.CompilerParams(vmem_limit_bytes=14 * 1024 * 1024),
        name="keep",
    )(in_scale, out_scale, own, in_raw, out_raw)
    return [pltpu.with_memory_space_constraint(h, pltpu.VMEM) for h in held]


def run_expert(blocks, owners, who, own, sib):
    tiles, width = own.shape[0], blocks[0].shape[1] - LANES
    sizes = tuple(x.shape[0] for x in blocks)
    m = sum(sizes)
    whole = pl.BlockSpec(memory_space=pltpu.VMEM)
    return pl.pallas_call(
        functools.partial(expert_kernel, sizes, owners),
        out_shape=[jax.ShapeDtypeStruct((size, width), jnp.bfloat16) for size in sizes],
        in_specs=[pl.BlockSpec(memory_space=pltpu.SMEM)]
        + [whole] * (2 + len(blocks)),
        out_specs=[whole] * len(blocks),
        scratch_shapes=[
            pltpu.VMEM((m, width), jnp.bfloat16),
            pltpu.VMEM((m, width), jnp.float32),
        ],
        compiler_params=pltpu.CompilerParams(vmem_limit_bytes=24 * 1024 * 1024),
        cost_estimate=cost(12 * m * width * tiles * TILE_F, 12 * width * tiles * TILE_F),
        name="expert",
    )(who, own, sib, *blocks)


def after(value, *others):
    return lax.optimization_barrier((value, others))[0]


def shards(order, tokens, expert_ids, combine, hot_list, in_weight, in_scale, out_weight, out_scale):
    owners = lax.axis_size("expert")
    halves = lax.axis_size("dp")
    tok_rows, width = tokens.shape
    capacity = tok_rows * expert_ids.shape[1] * 3 // (4 * owners)
    who = lax.axis_index("expert").astype(jnp.int32).reshape(1)
    far = owners // 2
    size = tok_rows // CHUNKS
    mid = size // 2
    chunks = range(CHUNKS)

    def shift(x, by, name):
        with jax.named_scope(name + ("_right" if by > 0 else "_left")):
            return lax.ppermute(
                x, "expert", [(order[i], order[(i + by) % owners]) for i in range(owners)]
            )

    def add(a, b):
        return (a.astype(jnp.float32) + b.astype(jnp.float32)).astype(jnp.bfloat16)

    have = [{}]
    done = [{} for _ in chunks]

    def gather(c, s):
        if s < far:
            have[c][-s] = shift(have[c][1 - s], 1, f"tokens_{c}_{s}")
            have[c][s] = shift(have[c][s - 1], -1, f"tokens_{c}_{s}")
        else:
            have[c]["top"] = shift(have[c][1 - s][:mid], 1, f"tokens_{c}_{s}")
            have[c]["bottom"] = shift(have[c][s - 1][mid:], -1, f"tokens_{c}_{s}")

    def expert(*keys):
        blocks = [have[c][key] for c, key in keys]
        for (c, key), out in zip(keys, run_expert(blocks, owners, who, own, sib)):
            done[c][key] = out

    def hold(keys, *others):
        for c, key in keys:
            have[c][key] = after(have[c][key], *others)

    def every(*steps):
        return [(c, key) for s in steps for c in chunks for key in ((s, -s) if s else (0,))]

    bare = {0: tokens, -1: shift(tokens, 1, "tokens_0_1"), 1: shift(tokens, -1, "tokens_0_1")}
    extra = {0: route(hot_list, expert_ids, combine, owners, capacity)}
    extra[-1] = shift(extra[0], 1, "weights_0_1")
    extra[1] = shift(extra[0], -1, "weights_0_1")
    for s in bare:
        have[0][s] = jnp.concatenate([bare[s], extra[s]], axis=1)
    raw = (in_weight[0], in_scale[0], out_weight[0], out_scale[0])
    sizes = jnp.concatenate([raw[1].reshape(-1), raw[3].reshape(-1)])

    def swap(w):
        return lax.ppermute(w, "dp", [(i, (i + 1) % halves) for i in range(halves)])

    sizes = swap(sizes)
    in_sib = swap(raw[0])
    own = dequantize(*after(raw, extra[0]))
    out_sib = swap(raw[2])
    for s in range(2, far):
        for c in chunks:
            if s == 2:
                hold([(c, 1), (c, -1)], own)
            gather(c, s)
    cut = raw[1].size
    own, sib = keep(
        own, in_sib, sizes[:cut].reshape(raw[1].shape), out_sib, sizes[cut:].reshape(raw[3].shape)
    )
    hold(every(far - 1), own)
    gather(0, far)
    expert((0, far - 1), (0, 1 - far))
    hold([(0, "top"), (0, "bottom")], done[0][far - 1])
    expert((0, "top"), (0, "bottom"))

    part = done[0]
    right_low = shift(part[far - 1][mid:], 1, f"sums_1_{far - 1}")
    left_top = shift(part[1 - far][:mid], -1, f"sums_1_{far - 1}")
    right_top = shift(part["top"], 1, f"sums_0_{far}")
    left_low = shift(part["bottom"], -1, f"sums_0_{far}")
    before = part["top"]
    for s in range(far - 1, 1, -1):
        keys = [(0, s - 1), (0, 1 - s)] + ([(0, 0)] if s == 2 else [])
        hold(keys, before)
        expert(*keys)
        before = right_top
        right = jnp.concatenate(
            [add(part[s][:mid], right_top), add(part[s - 1][mid:], right_low)], axis=0
        )
        left = jnp.concatenate(
            [add(part[1 - s][:mid], left_top), add(part[-s][mid:], left_low)], axis=0
        )
        right, left = shift(right, 1, f"sums_0_{s}"), shift(left, -1, f"sums_0_{s}")
        right_top, right_low = right[:mid], right[mid:]
        left_top, left_low = left[:mid], left[mid:]
    right_top = shift(add(part[1][:mid], right_top), 1, "sums_0_1")
    left_low = shift(add(part[-1][mid:], left_low), -1, "sums_0_1")

    def three(*terms):
        return sum(t.astype(jnp.float32) for t in terms).astype(jnp.bfloat16)

    return jnp.concatenate(
        [
            three(part[0][:mid], right_top, left_top),
            three(part[0][mid:], right_low, left_low),
        ],
        axis=0,
    )


def solution(mesh):
    placed = (
        P(("group", "expert", "dp"), None),
        P(("group", "expert", "dp"), None),
        P(("group", "expert", "dp"), None),
        P("group"),
        P("expert", None, None, "dp"),
        P("expert", None, None, "dp"),
        P("expert", "dp", None),
        P("expert", "dp", None),
    )
    return jax.shard_map(
        functools.partial(shards, ring_order(mesh)),
        mesh=mesh,
        in_specs=placed,
        out_specs=P(("group", "expert", "dp"), None),
        check_vma=False,
    )
```

```python
import functools

import jax
import jax.numpy as jnp
from jax import lax
from jax.experimental import pallas as pl
from jax.experimental.pallas import tpu as pltpu
from jax.sharding import PartitionSpec as P

QB = 128
TILE_F = 256
LANES = 128
VMEM_LIMIT = 56 * 1024 * 1024
CHUNKS = 1
SCALE = 1.0


def cost(flops, bytes_accessed):
    return pl.CostEstimate(
        flops=int(flops * SCALE), bytes_accessed=int(bytes_accessed * SCALE), transcendentals=0
    )


def ring_order(mesh):
    count = mesh.shape["expert"]
    rows = 2 if count == 8 else 1
    first = [i * rows for i in range(count // rows)]
    second = [i * rows + 1 for i in reversed(range(count // rows))] if rows == 2 else []
    return first + second


def dequantize_kernel(in_scale, out_scale, in_raw, out_raw, out_ref):
    f, part = pl.program_id(0), pl.program_id(1)
    chunk = in_raw.shape[1]

    def scaled(block, scale):
        return (block.astype(jnp.float32) * scale).astype(jnp.bfloat16)

    @pl.when(part < 2)
    def _():
        for side in range(2):
            for i in range(chunk // QB):
                for j in range(TILE_F // QB):
                    scale = in_scale[side, part * (chunk // QB) + i, f * (TILE_F // QB) + j]
                    at = side * TILE_F + j * QB
                    out_ref[0, i * QB : (i + 1) * QB, at : at + QB] = scaled(
                        in_raw[side, i * QB : (i + 1) * QB, j * QB : (j + 1) * QB], scale
                    )

    @pl.when(part == 2)
    def _():
        per = 2 * TILE_F // QB
        for i in range(TILE_F // QB):
            for j in range(out_raw.shape[1] // QB):
                scale = out_scale[f * (TILE_F // QB) + i, j]
                row, at = (j // per) * TILE_F + i * QB, (j % per) * QB
                out_ref[0, row : row + QB, at : at + QB] = scaled(
                    out_raw[i * QB : (i + 1) * QB, j * QB : (j + 1) * QB], scale
                )


def dequantize(in_raw, in_scale, out_raw, out_scale):
    width, half = in_raw.shape[1], in_raw.shape[2]
    tiles = half // TILE_F
    chunk = width // 2
    return pl.pallas_call(
        dequantize_kernel,
        grid=(tiles, 3),
        out_shape=jax.ShapeDtypeStruct((tiles, 3 * chunk, 2 * TILE_F), jnp.bfloat16),
        in_specs=[
            pl.BlockSpec(memory_space=pltpu.SMEM),
            pl.BlockSpec(memory_space=pltpu.SMEM),
            pl.BlockSpec((2, chunk, TILE_F), lambda f, p: (0, jnp.minimum(p, 1), f)),
            pl.BlockSpec((TILE_F, width), lambda f, p: (f, 0)),
        ],
        out_specs=pl.BlockSpec((1, chunk, 2 * TILE_F), lambda f, p: (f, p, 0)),
        compiler_params=pltpu.CompilerParams(vmem_limit_bytes=24 * 1024 * 1024),
        cost_estimate=cost(6 * width * half, 12 * width * half),
        name="dequantize",
    )(in_scale, out_scale, in_raw, out_raw)


def route_kernel(capacity, owners, hot_ref, ids_ref, combine_ref, out_ref):
    picks, rows = ids_ref.shape
    expert = lax.broadcasted_iota(jnp.int32, (owners, rows), 0)
    named = jnp.zeros((owners, rows), jnp.float32)
    weight = jnp.zeros((owners, rows), jnp.float32)
    for k in range(picks):
        here = ids_ref[k : k + 1, :] == expert
        named = named + jnp.where(here, 1.0, 0.0)
        weight = weight + jnp.where(here, combine_ref[k : k + 1, :], 0.0)
    earlier = lax.broadcasted_iota(jnp.int32, (rows, rows), 0)
    later = lax.broadcasted_iota(jnp.int32, (rows, rows), 1)
    before = jnp.where(earlier < later, 1.0, 0.0).astype(jnp.bfloat16)
    rank = jnp.dot(named.astype(jnp.bfloat16), before, preferred_element_type=jnp.float32)
    weight = jnp.where((expert == hot_ref[0]) | (rank < capacity), weight, 0.0)
    pieces = []
    for _ in range(3):
        piece = weight.astype(jnp.bfloat16).astype(jnp.float32)
        weight = weight - piece
        pieces.append(piece)
    pieces.append(jnp.zeros((LANES - 3 * owners, rows), jnp.float32))
    extra = jnp.concatenate(pieces, axis=0).T.astype(jnp.bfloat16)
    out_ref[...] = extra


def route(hot_list, expert_ids, combine, owners, capacity):
    rows = expert_ids.shape[0]
    vmem = pl.BlockSpec(memory_space=pltpu.VMEM)
    return pl.pallas_call(
        functools.partial(route_kernel, capacity, owners),
        out_shape=jax.ShapeDtypeStruct((rows, LANES), jnp.bfloat16),
        in_specs=[pl.BlockSpec(memory_space=pltpu.SMEM), vmem, vmem],
        out_specs=vmem,
        name="route",
    )(hot_list, expert_ids.T, combine.T)


def expert_kernel(sizes, owners, who_ref, own, sib, *refs):
    blocks = len(sizes)
    x_refs, o_refs = refs[:blocks], refs[blocks : 2 * blocks]
    rows, total = refs[2 * blocks :]
    starts = [sum(sizes[:i]) for i in range(blocks)]
    half_tiles, width = own.shape[0], rows.shape[1]
    tiles = 2 * half_tiles
    for start, size, x_ref in zip(starts, sizes, x_refs):
        rows[start : start + size, :] = x_ref[:, :width]

    for tile in range(tiles):
        held, at = (own, tile) if tile < half_tiles else (sib, tile - half_tiles)
        both = jnp.dot(rows[...], held[at, :width], preferred_element_type=jnp.float32)
        gate, up = both[:, :TILE_F], both[:, TILE_F:]
        hidden = (gate / (1.0 + jnp.exp(-gate)) * up).astype(jnp.bfloat16)
        for i in range(width // (2 * TILE_F)):
            to = slice(i * 2 * TILE_F, (i + 1) * 2 * TILE_F)
            term = jnp.dot(
                hidden,
                held[at, width + i * TILE_F : width + (i + 1) * TILE_F],
                preferred_element_type=jnp.float32,
            )
            total[:, to] = term if tile == 0 else total[:, to] + term
    for start, size, x_ref, o_ref in zip(starts, sizes, x_refs, o_refs):
        lane = lax.broadcasted_iota(jnp.int32, (size, LANES), 1)
        picked = (lax.rem(lane, owners) == who_ref[0]) & (lane < 3 * owners)
        weight = jnp.where(picked, x_ref[:, width:].astype(jnp.float32), 0.0)
        weight = jnp.sum(weight, axis=1, keepdims=True)
        o_ref[...] = (total[start : start + size, :] * weight).astype(jnp.bfloat16)


def keep_kernel(
    in_scale, out_scale, own_from, in_raw, out_raw, own_to, sib_to, in_here, out_here, own_sem, in_sem, out_sem
):
    tiles, width = own_from.shape[0], in_raw.shape[1]
    parts = 4
    chunk = width // parts

    def in_copy(part):
        rows = pl.ds(pl.multiple_of(part * chunk, QB), chunk)
        return pltpu.make_async_copy(in_raw.at[:, rows], in_here.at[:, rows], in_sem.at[part])

    out_copy = pltpu.make_async_copy(out_raw, out_here, out_sem)
    own_copies = [
        pltpu.make_async_copy(own_from.at[tile], own_to.at[tile], own_sem.at[tile])
        for tile in range(tiles)
    ]
    for part in range(parts):
        in_copy(part).start()
    out_copy.start()
    for copy in own_copies:
        copy.start()

    def scaled(block, scale):
        return (block.astype(jnp.float32) * scale).astype(jnp.bfloat16)

    def gate_up(part, carry):
        in_copy(part).wait()
        for i in range(chunk // QB):
            row = part * (chunk // QB) + i
            rows = pl.ds(pl.multiple_of(row * QB, QB), QB)
            for side in range(2):
                for j in range(tiles * TILE_F // QB):
                    tile, at = (j * QB) // TILE_F, side * TILE_F + (j * QB) % TILE_F
                    sib_to[tile, rows, at : at + QB] = scaled(
                        in_here[side, rows, j * QB : (j + 1) * QB], in_scale[side, row, j]
                    )
        return carry

    lax.fori_loop(0, parts, gate_up, 0)
    out_copy.wait()
    per = 2 * TILE_F // QB
    below = TILE_F // QB

    def down(i, carry):
        rows = pl.ds(pl.multiple_of(i * QB, QB), QB)
        for j in range(width // QB):
            to = width + (j // per) * TILE_F + lax.rem(i, below) * QB
            at = (j % per) * QB
            sib_to[lax.div(i, below), pl.ds(pl.multiple_of(to, QB), QB), at : at + QB] = scaled(
                out_here[rows, j * QB : (j + 1) * QB], out_scale[i, j]
            )
        return carry

    lax.fori_loop(0, tiles * below, down, 0)
    for copy in own_copies:
        copy.wait()


def keep(own, in_raw, in_scale, out_raw, out_scale):
    smem = pl.BlockSpec(memory_space=pltpu.SMEM)
    held = pl.pallas_call(
        keep_kernel,
        out_shape=[pltpu.VMEM(own.shape, own.dtype)] * 2,
        in_specs=[smem, smem] + [pl.BlockSpec(memory_space=pl.ANY)] * 3,
        out_specs=[pl.BlockSpec(memory_space=pltpu.VMEM)] * 2,
        scratch_shapes=[
            pltpu.VMEM(in_raw.shape, in_raw.dtype),
            pltpu.VMEM(out_raw.shape, out_raw.dtype),
            pltpu.SemaphoreType.DMA((own.shape[0],)),
            pltpu.SemaphoreType.DMA((4,)),
            pltpu.SemaphoreType.DMA(()),
        ],
        compiler_params=pltpu.CompilerParams(vmem_limit_bytes=14 * 1024 * 1024),
        name="keep",
    )(in_scale, out_scale, own, in_raw, out_raw)
    return [pltpu.with_memory_space_constraint(h, pltpu.VMEM) for h in held]


def run_expert(blocks, owners, who, own, sib):
    tiles, width = own.shape[0], blocks[0].shape[1] - LANES
    sizes = tuple(x.shape[0] for x in blocks)
    m = sum(sizes)
    whole = pl.BlockSpec(memory_space=pltpu.VMEM)
    return pl.pallas_call(
        functools.partial(expert_kernel, sizes, owners),
        out_shape=[jax.ShapeDtypeStruct((size, width), jnp.bfloat16) for size in sizes],
        in_specs=[pl.BlockSpec(memory_space=pltpu.SMEM)]
        + [whole] * (2 + len(blocks)),
        out_specs=[whole] * len(blocks),
        scratch_shapes=[
            pltpu.VMEM((m, width), jnp.bfloat16),
            pltpu.VMEM((m, width), jnp.float32),
        ],
        compiler_params=pltpu.CompilerParams(vmem_limit_bytes=24 * 1024 * 1024),
        cost_estimate=cost(12 * m * width * tiles * TILE_F, 12 * width * tiles * TILE_F),
        name="expert",
    )(who, own, sib, *blocks)


def after(value, *others):
    return lax.optimization_barrier((value, others))[0]


def shards(order, tokens, expert_ids, combine, hot_list, in_weight, in_scale, out_weight, out_scale):
    owners = lax.axis_size("expert")
    halves = lax.axis_size("dp")
    tok_rows, width = tokens.shape
    capacity = tok_rows * expert_ids.shape[1] * 3 // (4 * owners)
    who = lax.axis_index("expert").astype(jnp.int32).reshape(1)
    far = owners // 2
    size = tok_rows // CHUNKS
    mid = size // 2
    chunks = range(CHUNKS)

    def shift(x, by, name):
        with jax.named_scope(name + ("_right" if by > 0 else "_left")):
            return lax.ppermute(
                x, "expert", [(order[i], order[(i + by) % owners]) for i in range(owners)]
            )

    def add(a, b):
        return (a.astype(jnp.float32) + b.astype(jnp.float32)).astype(jnp.bfloat16)

    have = [{}]
    done = [{} for _ in chunks]

    def gather(c, s):
        if s < far:
            have[c][-s] = shift(have[c][1 - s], 1, f"tokens_{c}_{s}")
            have[c][s] = shift(have[c][s - 1], -1, f"tokens_{c}_{s}")
        else:
            have[c]["top"] = shift(have[c][1 - s][:mid], 1, f"tokens_{c}_{s}")
            have[c]["bottom"] = shift(have[c][s - 1][mid:], -1, f"tokens_{c}_{s}")

    def expert(*keys):
        blocks = [have[c][key] for c, key in keys]
        for (c, key), out in zip(keys, run_expert(blocks, owners, who, own, sib)):
            done[c][key] = out

    def hold(keys, *others):
        for c, key in keys:
            have[c][key] = after(have[c][key], *others)

    def every(*steps):
        return [(c, key) for s in steps for c in chunks for key in ((s, -s) if s else (0,))]

    bare = {0: tokens, -1: shift(tokens, 1, "tokens_0_1"), 1: shift(tokens, -1, "tokens_0_1")}
    extra = {0: route(hot_list, expert_ids, combine, owners, capacity)}
    extra[-1] = shift(extra[0], 1, "weights_0_1")
    extra[1] = shift(extra[0], -1, "weights_0_1")
    for s in bare:
        have[0][s] = jnp.concatenate([bare[s], extra[s]], axis=1)
    raw = (in_weight[0], in_scale[0], out_weight[0], out_scale[0])
    sizes = jnp.concatenate([raw[1].reshape(-1), raw[3].reshape(-1)])

    def swap(w):
        return lax.ppermute(w, "dp", [(i, (i + 1) % halves) for i in range(halves)])

    sizes = swap(sizes)
    in_sib = swap(raw[0])
    own = dequantize(*after(raw, extra[0]))
    out_sib = swap(raw[2])
    for s in range(2, far):
        for c in chunks:
            if s == 3:
                hold([(c, 2), (c, -2)], own)
            gather(c, s)
    cut = raw[1].size
    own, sib = keep(
        own, in_sib, sizes[:cut].reshape(raw[1].shape), out_sib, sizes[cut:].reshape(raw[3].shape)
    )
    hold(every(far - 1), own)
    gather(0, far)
    expert((0, far - 1), (0, 1 - far))
    hold([(0, "top"), (0, "bottom")], done[0][far - 1])
    expert((0, "top"), (0, "bottom"))

    part = done[0]
    right_low = shift(part[far - 1][mid:], 1, f"sums_1_{far - 1}")
    left_top = shift(part[1 - far][:mid], -1, f"sums_1_{far - 1}")
    right_top = shift(part["top"], 1, f"sums_0_{far}")
    left_low = shift(part["bottom"], -1, f"sums_0_{far}")
    before = part["top"]
    for s in range(far - 1, 1, -1):
        keys = [(0, s - 1), (0, 1 - s)] + ([(0, 0)] if s == 2 else [])
        hold(keys, before)
        expert(*keys)
        before = right_top
        right = jnp.concatenate(
            [add(part[s][:mid], right_top), add(part[s - 1][mid:], right_low)], axis=0
        )
        left = jnp.concatenate(
            [add(part[1 - s][:mid], left_top), add(part[-s][mid:], left_low)], axis=0
        )
        right, left = shift(right, 1, f"sums_0_{s}"), shift(left, -1, f"sums_0_{s}")
        right_top, right_low = right[:mid], right[mid:]
        left_top, left_low = left[:mid], left[mid:]
    right_top = shift(add(part[1][:mid], right_top), 1, "sums_0_1")
    left_low = shift(add(part[-1][mid:], left_low), -1, "sums_0_1")

    def three(*terms):
        return sum(t.astype(jnp.float32) for t in terms).astype(jnp.bfloat16)

    return jnp.concatenate(
        [
            three(part[0][:mid], right_top, left_top),
            three(part[0][mid:], right_low, left_low),
        ],
        axis=0,
    )


def solution(mesh):
    placed = (
        P(("group", "expert", "dp"), None),
        P(("group", "expert", "dp"), None),
        P(("group", "expert", "dp"), None),
        P("group"),
        P("expert", None, None, "dp"),
        P("expert", None, None, "dp"),
        P("expert", "dp", None),
        P("expert", "dp", None),
    )
    return jax.shard_map(
        functools.partial(shards, ring_order(mesh)),
        mesh=mesh,
        in_specs=placed,
        out_specs=P(("group", "expert", "dp"), None),
        check_vma=False,
    )
```

```python
import functools

import jax
import jax.numpy as jnp
from jax import lax
from jax.experimental import pallas as pl
from jax.experimental.pallas import tpu as pltpu
from jax.sharding import PartitionSpec as P

QB = 128
TILE_F = 256
LANES = 128
VMEM_LIMIT = 56 * 1024 * 1024
CHUNKS = 1
SCALE = 1.0


def cost(flops, bytes_accessed):
    return pl.CostEstimate(
        flops=int(flops * SCALE), bytes_accessed=int(bytes_accessed * SCALE), transcendentals=0
    )


def ring_order(mesh):
    count = mesh.shape["expert"]
    rows = 2 if count == 8 else 1
    first = [i * rows for i in range(count // rows)]
    second = [i * rows + 1 for i in reversed(range(count // rows))] if rows == 2 else []
    return first + second


def dequantize_kernel(in_scale, out_scale, in_raw, out_raw, out_ref):
    f, part = pl.program_id(0), pl.program_id(1)
    chunk = in_raw.shape[1]

    def scaled(block, scale):
        return (block.astype(jnp.float32) * scale).astype(jnp.bfloat16)

    @pl.when(part < 2)
    def _():
        for side in range(2):
            for i in range(chunk // QB):
                for j in range(TILE_F // QB):
                    scale = in_scale[side, part * (chunk // QB) + i, f * (TILE_F // QB) + j]
                    at = side * TILE_F + j * QB
                    out_ref[0, i * QB : (i + 1) * QB, at : at + QB] = scaled(
                        in_raw[side, i * QB : (i + 1) * QB, j * QB : (j + 1) * QB], scale
                    )

    @pl.when(part == 2)
    def _():
        per = 2 * TILE_F // QB
        for i in range(TILE_F // QB):
            for j in range(out_raw.shape[1] // QB):
                scale = out_scale[f * (TILE_F // QB) + i, j]
                row, at = (j // per) * TILE_F + i * QB, (j % per) * QB
                out_ref[0, row : row + QB, at : at + QB] = scaled(
                    out_raw[i * QB : (i + 1) * QB, j * QB : (j + 1) * QB], scale
                )


def dequantize(in_raw, in_scale, out_raw, out_scale):
    width, half = in_raw.shape[1], in_raw.shape[2]
    tiles = half // TILE_F
    chunk = width // 2
    return pl.pallas_call(
        dequantize_kernel,
        grid=(tiles, 3),
        out_shape=jax.ShapeDtypeStruct((tiles, 3 * chunk, 2 * TILE_F), jnp.bfloat16),
        in_specs=[
            pl.BlockSpec(memory_space=pltpu.SMEM),
            pl.BlockSpec(memory_space=pltpu.SMEM),
            pl.BlockSpec((2, chunk, TILE_F), lambda f, p: (0, jnp.minimum(p, 1), f)),
            pl.BlockSpec((TILE_F, width), lambda f, p: (f, 0)),
        ],
        out_specs=pl.BlockSpec((1, chunk, 2 * TILE_F), lambda f, p: (f, p, 0)),
        compiler_params=pltpu.CompilerParams(vmem_limit_bytes=24 * 1024 * 1024),
        cost_estimate=cost(6 * width * half, 12 * width * half),
        name="dequantize",
    )(in_scale, out_scale, in_raw, out_raw)


def route_kernel(capacity, owners, hot_ref, ids_ref, combine_ref, out_ref):
    picks, rows = ids_ref.shape
    expert = lax.broadcasted_iota(jnp.int32, (owners, rows), 0)
    named = jnp.zeros((owners, rows), jnp.float32)
    weight = jnp.zeros((owners, rows), jnp.float32)
    for k in range(picks):
        here = ids_ref[k : k + 1, :] == expert
        named = named + jnp.where(here, 1.0, 0.0)
        weight = weight + jnp.where(here, combine_ref[k : k + 1, :], 0.0)
    earlier = lax.broadcasted_iota(jnp.int32, (rows, rows), 0)
    later = lax.broadcasted_iota(jnp.int32, (rows, rows), 1)
    before = jnp.where(earlier < later, 1.0, 0.0).astype(jnp.bfloat16)
    rank = jnp.dot(named.astype(jnp.bfloat16), before, preferred_element_type=jnp.float32)
    weight = jnp.where((expert == hot_ref[0]) | (rank < capacity), weight, 0.0)
    pieces = []
    for _ in range(3):
        piece = weight.astype(jnp.bfloat16).astype(jnp.float32)
        weight = weight - piece
        pieces.append(piece)
    pieces.append(jnp.zeros((LANES - 3 * owners, rows), jnp.float32))
    extra = jnp.concatenate(pieces, axis=0).T.astype(jnp.bfloat16)
    out_ref[...] = extra


def route(hot_list, expert_ids, combine, owners, capacity):
    rows = expert_ids.shape[0]
    vmem = pl.BlockSpec(memory_space=pltpu.VMEM)
    return pl.pallas_call(
        functools.partial(route_kernel, capacity, owners),
        out_shape=jax.ShapeDtypeStruct((rows, LANES), jnp.bfloat16),
        in_specs=[pl.BlockSpec(memory_space=pltpu.SMEM), vmem, vmem],
        out_specs=vmem,
        name="route",
    )(hot_list, expert_ids.T, combine.T)


def expert_kernel(sizes, owners, who_ref, own, sib, *refs):
    blocks = len(sizes)
    x_refs, o_refs = refs[:blocks], refs[blocks : 2 * blocks]
    rows, total = refs[2 * blocks :]
    starts = [sum(sizes[:i]) for i in range(blocks)]
    half_tiles, width = own.shape[0], rows.shape[1]
    tiles = 2 * half_tiles
    for start, size, x_ref in zip(starts, sizes, x_refs):
        rows[start : start + size, :] = x_ref[:, :width]

    for tile in range(tiles):
        held, at = (own, tile) if tile < half_tiles else (sib, tile - half_tiles)
        both = jnp.dot(rows[...], held[at, :width], preferred_element_type=jnp.float32)
        gate, up = both[:, :TILE_F], both[:, TILE_F:]
        hidden = (gate / (1.0 + jnp.exp(-gate)) * up).astype(jnp.bfloat16)
        for i in range(width // (2 * TILE_F)):
            to = slice(i * 2 * TILE_F, (i + 1) * 2 * TILE_F)
            term = jnp.dot(
                hidden,
                held[at, width + i * TILE_F : width + (i + 1) * TILE_F],
                preferred_element_type=jnp.float32,
            )
            total[:, to] = term if tile == 0 else total[:, to] + term
    for start, size, x_ref, o_ref in zip(starts, sizes, x_refs, o_refs):
        lane = lax.broadcasted_iota(jnp.int32, (size, LANES), 1)
        picked = (lax.rem(lane, owners) == who_ref[0]) & (lane < 3 * owners)
        weight = jnp.where(picked, x_ref[:, width:].astype(jnp.float32), 0.0)
        weight = jnp.sum(weight, axis=1, keepdims=True)
        o_ref[...] = (total[start : start + size, :] * weight).astype(jnp.bfloat16)


def keep_kernel(
    in_scale, out_scale, own_from, in_raw, out_raw, own_to, sib_to, in_here, out_here, own_sem, in_sem, out_sem
):
    tiles, width = own_from.shape[0], in_raw.shape[1]
    parts = 4
    chunk = width // parts

    def in_copy(part):
        rows = pl.ds(pl.multiple_of(part * chunk, QB), chunk)
        return pltpu.make_async_copy(in_raw.at[:, rows], in_here.at[:, rows], in_sem.at[part])

    out_copy = pltpu.make_async_copy(out_raw, out_here, out_sem)
    own_copies = [
        pltpu.make_async_copy(own_from.at[tile], own_to.at[tile], own_sem.at[tile])
        for tile in range(tiles)
    ]
    for part in range(parts):
        in_copy(part).start()
    out_copy.start()
    for copy in own_copies:
        copy.start()

    def scaled(block, scale):
        return (block.astype(jnp.float32) * scale).astype(jnp.bfloat16)

    def gate_up(part, carry):
        in_copy(part).wait()
        for i in range(chunk // QB):
            row = part * (chunk // QB) + i
            rows = pl.ds(pl.multiple_of(row * QB, QB), QB)
            for side in range(2):
                for j in range(tiles * TILE_F // QB):
                    tile, at = (j * QB) // TILE_F, side * TILE_F + (j * QB) % TILE_F
                    sib_to[tile, rows, at : at + QB] = scaled(
                        in_here[side, rows, j * QB : (j + 1) * QB], in_scale[side, row, j]
                    )
        return carry

    lax.fori_loop(0, parts, gate_up, 0)
    out_copy.wait()
    per = 2 * TILE_F // QB
    below = TILE_F // QB

    def down(i, carry):
        rows = pl.ds(pl.multiple_of(i * QB, QB), QB)
        for j in range(width // QB):
            to = width + (j // per) * TILE_F + lax.rem(i, below) * QB
            at = (j % per) * QB
            sib_to[lax.div(i, below), pl.ds(pl.multiple_of(to, QB), QB), at : at + QB] = scaled(
                out_here[rows, j * QB : (j + 1) * QB], out_scale[i, j]
            )
        return carry

    lax.fori_loop(0, tiles * below, down, 0)
    for copy in own_copies:
        copy.wait()


def keep(own, in_raw, in_scale, out_raw, out_scale):
    smem = pl.BlockSpec(memory_space=pltpu.SMEM)
    held = pl.pallas_call(
        keep_kernel,
        out_shape=[pltpu.VMEM(own.shape, own.dtype)] * 2,
        in_specs=[smem, smem] + [pl.BlockSpec(memory_space=pl.ANY)] * 3,
        out_specs=[pl.BlockSpec(memory_space=pltpu.VMEM)] * 2,
        scratch_shapes=[
            pltpu.VMEM(in_raw.shape, in_raw.dtype),
            pltpu.VMEM(out_raw.shape, out_raw.dtype),
            pltpu.SemaphoreType.DMA((own.shape[0],)),
            pltpu.SemaphoreType.DMA((4,)),
            pltpu.SemaphoreType.DMA(()),
        ],
        compiler_params=pltpu.CompilerParams(vmem_limit_bytes=14 * 1024 * 1024),
        name="keep",
    )(in_scale, out_scale, own, in_raw, out_raw)
    return [pltpu.with_memory_space_constraint(h, pltpu.VMEM) for h in held]


def run_expert(blocks, owners, who, own, sib):
    tiles, width = own.shape[0], blocks[0].shape[1] - LANES
    sizes = tuple(x.shape[0] for x in blocks)
    m = sum(sizes)
    whole = pl.BlockSpec(memory_space=pltpu.VMEM)
    return pl.pallas_call(
        functools.partial(expert_kernel, sizes, owners),
        out_shape=[jax.ShapeDtypeStruct((size, width), jnp.bfloat16) for size in sizes],
        in_specs=[pl.BlockSpec(memory_space=pltpu.SMEM)]
        + [whole] * (2 + len(blocks)),
        out_specs=[whole] * len(blocks),
        scratch_shapes=[
            pltpu.VMEM((m, width), jnp.bfloat16),
            pltpu.VMEM((m, width), jnp.float32),
        ],
        compiler_params=pltpu.CompilerParams(vmem_limit_bytes=24 * 1024 * 1024),
        cost_estimate=cost(12 * m * width * tiles * TILE_F, 12 * width * tiles * TILE_F),
        name="expert",
    )(who, own, sib, *blocks)


def after(value, *others):
    return lax.optimization_barrier((value, others))[0]


def shards(order, tokens, expert_ids, combine, hot_list, in_weight, in_scale, out_weight, out_scale):
    owners = lax.axis_size("expert")
    halves = lax.axis_size("dp")
    tok_rows, width = tokens.shape
    capacity = tok_rows * expert_ids.shape[1] * 3 // (4 * owners)
    who = lax.axis_index("expert").astype(jnp.int32).reshape(1)
    far = owners // 2
    size = tok_rows // CHUNKS
    mid = size // 2
    chunks = range(CHUNKS)

    def shift(x, by, name):
        with jax.named_scope(name + ("_right" if by > 0 else "_left")):
            return lax.ppermute(
                x, "expert", [(order[i], order[(i + by) % owners]) for i in range(owners)]
            )

    def add(a, b):
        return (a.astype(jnp.float32) + b.astype(jnp.float32)).astype(jnp.bfloat16)

    have = [{}]
    done = [{} for _ in chunks]

    def gather(c, s):
        if s < far:
            have[c][-s] = shift(have[c][1 - s], 1, f"tokens_{c}_{s}")
            have[c][s] = shift(have[c][s - 1], -1, f"tokens_{c}_{s}")
        else:
            have[c]["top"] = shift(have[c][1 - s][:mid], 1, f"tokens_{c}_{s}")
            have[c]["bottom"] = shift(have[c][s - 1][mid:], -1, f"tokens_{c}_{s}")

    def expert(*keys):
        blocks = [have[c][key] for c, key in keys]
        for (c, key), out in zip(keys, run_expert(blocks, owners, who, own, sib)):
            done[c][key] = out

    def hold(keys, *others):
        for c, key in keys:
            have[c][key] = after(have[c][key], *others)

    def every(*steps):
        return [(c, key) for s in steps for c in chunks for key in ((s, -s) if s else (0,))]

    bare = {0: tokens, -1: shift(tokens, 1, "tokens_0_1"), 1: shift(tokens, -1, "tokens_0_1")}
    extra = {0: route(hot_list, expert_ids, combine, owners, capacity)}
    extra[-1] = shift(extra[0], 1, "weights_0_1")
    extra[1] = shift(extra[0], -1, "weights_0_1")
    for s in bare:
        have[0][s] = jnp.concatenate([bare[s], extra[s]], axis=1)
    raw = (in_weight[0], in_scale[0], out_weight[0], out_scale[0])
    sizes = jnp.concatenate([raw[1].reshape(-1), raw[3].reshape(-1)])

    def swap(w):
        return lax.ppermute(w, "dp", [(i, (i + 1) % halves) for i in range(halves)])

    sizes = swap(sizes)
    in_sib = swap(raw[0])
    own = dequantize(*after(raw, extra[0]))
    out_sib = swap(raw[2])
    for s in range(2, far):
        for c in chunks:
            if s == 3:
                hold([(c, 2), (c, -2)], own)
            gather(c, s)
    cut = raw[1].size
    own, sib = keep(
        own, in_sib, sizes[:cut].reshape(raw[1].shape), out_sib, sizes[cut:].reshape(raw[3].shape)
    )
    hold(every(far - 1), own)
    gather(0, far)
    expert((0, far - 1), (0, 1 - far))
    hold([(0, "top"), (0, "bottom")], done[0][far - 1])
    expert((0, "top"), (0, "bottom"))

    part = done[0]
    right_low = shift(part[far - 1][mid:], 1, f"sums_1_{far - 1}")
    left_top = shift(part[1 - far][:mid], -1, f"sums_1_{far - 1}")
    right_top = shift(part["top"], 1, f"sums_0_{far}")
    left_low = shift(part["bottom"], -1, f"sums_0_{far}")
    before = part["top"]
    for s in range(far - 1, 1, -1):
        keys = [(0, s - 1), (0, 1 - s)]
        hold(keys, before)
        expert(*keys)
        before = right_top
        right = jnp.concatenate(
            [add(part[s][:mid], right_top), add(part[s - 1][mid:], right_low)], axis=0
        )
        left = jnp.concatenate(
            [add(part[1 - s][:mid], left_top), add(part[-s][mid:], left_low)], axis=0
        )
        right, left = shift(right, 1, f"sums_0_{s}"), shift(left, -1, f"sums_0_{s}")
        right_top, right_low = right[:mid], right[mid:]
        left_top, left_low = left[:mid], left[mid:]
    hold([(0, 0)], right_top)
    expert((0, 0))
    right_top = shift(add(part[1][:mid], right_top), 1, "sums_0_1")
    left_low = shift(add(part[-1][mid:], left_low), -1, "sums_0_1")

    def three(*terms):
        return sum(t.astype(jnp.float32) for t in terms).astype(jnp.bfloat16)

    return jnp.concatenate(
        [
            three(part[0][:mid], right_top, left_top),
            three(part[0][mid:], right_low, left_low),
        ],
        axis=0,
    )


def solution(mesh):
    placed = (
        P(("group", "expert", "dp"), None),
        P(("group", "expert", "dp"), None),
        P(("group", "expert", "dp"), None),
        P("group"),
        P("expert", None, None, "dp"),
        P("expert", None, None, "dp"),
        P("expert", "dp", None),
        P("expert", "dp", None),
    )
    return jax.shard_map(
        functools.partial(shards, ring_order(mesh)),
        mesh=mesh,
        in_specs=placed,
        out_specs=P(("group", "expert", "dp"), None),
        check_vma=False,
    )
```
